32 devices in a mesh: groups: 2 (over x), chan: 16 (over z, y, core).
Axes of the slice: x: 2, y: 2, z: 4, core: 2. Of those that a mesh axis runs over, the one named last changes fastest.
Arguments:
- raw_strain: bfloat16 [8, 512, 4096], P(None, ('groups', 'chan')), parts along dimension 1, may hold values from -60 to 60
- bandpass: bfloat16 [64], replicated, may hold values from -0.75 to 0.75
- whiten_taps: bfloat16 [512, 64], P(('groups', 'chan')), parts along dimension 0, may hold values from -0.75 to 0.75
- segment_mask: int32 [8, 512], P(None, 'groups'), parts along dimension 1, may hold values from 0 to 1, as said below
- channel_block: int32 [512], P('groups'), parts along dimension 0, may hold values from 0 to 1, as said below
- source_block: int32 [2], P('groups'), parts along dimension 0, may hold values from 0 to 1
Outputs:
- correlations: bfloat16 [128, 512, 1024], P(None, ('groups', 'chan')), parts along dimension 1
The draws below stay inside these ranges and needn't reach their ends.
There are 2 independent parts, one for each index of `groups`. The reference program is written for one: setup_inputs(seed, part) draws one part's arguments, and reference() takes and returns one part's arrays. A program takes and returns all parts, laid end to end along the dimension named above; an argument that names none is the same for every part. Nothing has to cross between parts.
Inputs may be any that keep to these rules, and one draw needn't show every extreme that they name: `segment_mask`: 1 marks a usable segment of a channel; some channels have no usable segment. `channel_block`: each block number is held by exactly 128 channels.
All inputs are finite; a program needn't handle non-finite values.
Results may differ from the reference program's by a relative error of at most 0.0093.
Values may be sent and summed in bfloat16 or wider, within the bound.
A program may use at most 64 MiB of HBM per device.

```python
import math
import jax
import jax.numpy as jnp
from jax import lax

SAMPLES = 4096
TAPS = 64
KLO = 64
FBINS = 512
LAGS = 1024
BLOCK = 128
SEGS = 8
CHANNELS = 256


def draw_raw_strain(key, part):
    noise_key, level_key = jax.random.split(key)
    noise = jnp.clip(jax.random.normal(noise_key, (SEGS, CHANNELS, SAMPLES), jnp.float32), -6.0, 6.0)
    level = jnp.exp(jax.random.uniform(level_key, (SEGS, CHANNELS, 1), jnp.float32, 0.0, math.log(10.0)))
    return (noise * level).astype(jnp.bfloat16)


def draw_segment_mask(key, part):
    usable_key, alive_key, dead_key = jax.random.split(key, 3)
    usable = jax.random.randint(usable_key, (SEGS, CHANNELS), 0, 4) > 0
    alive = jax.random.randint(alive_key, (1, CHANNELS), 0, 16) > 0
    dead_one = jax.random.randint(dead_key, (), 0, CHANNELS)
    alive = alive & (jnp.arange(CHANNELS, dtype=jnp.int32)[None, :] != dead_one)
    return (usable & alive).astype(jnp.int32)


def draw_channel_block(key, part):
    return (jax.random.permutation(key, CHANNELS) // BLOCK).astype(jnp.int32)


def block_scale(rng, shape, cuts, least, largest):
    factor_of, own = 1.0, jax.random.fold_in(rng, 6)
    for dim, shards_of in cuts:
        heights = jnp.exp(jax.random.uniform(jax.random.fold_in(own, dim), (shards_of,), jnp.float32, least / len(cuts), largest / len(cuts)))
        factor_of = factor_of * jnp.repeat(heights, shape[dim] // shards_of).reshape([-1 if axis == dim else 1 for axis in range(len(shape))])
    return factor_of


def normal_values(stream_key, shape, scale, bound, cuts=(), held_as=jnp.bfloat16):
    values = jax.random.normal(stream_key, shape, jnp.float32) * scale
    if len(cuts) > 0:
        values = block_scale(stream_key, shape, cuts, -0.22, 0.18) * values
    return jnp.clip(values, min=-bound, max=bound).astype(held_as)


def setup_inputs(seed: int = 0, part: int = 0) -> dict:
    key_list = jax.random.split(jax.random.key(seed), 7)
    part_keys = jax.random.split(jax.random.fold_in(key_list[6], part), 7)
    return {
        "raw_strain": draw_raw_strain(jax.random.fold_in(jax.random.fold_in(key_list[6], part), 71), part),
        "bandpass": normal_values(key_list[1], (TAPS,), TAPS ** -0.5, 0.75),
        "whiten_taps": normal_values(part_keys[2], (CHANNELS, TAPS), TAPS ** -0.5, 0.75, ((0, 16),)),
        "segment_mask": draw_segment_mask(jax.random.fold_in(jax.random.fold_in(key_list[6], part), 71), part),
        "channel_block": draw_channel_block(jax.random.fold_in(jax.random.fold_in(key_list[6], part), 71), part),
        "source_block": jax.random.randint(part_keys[5], (1,), 0, CHANNELS // BLOCK).astype(jnp.int32),
    }


def fir_matrix(coeffs):
    inner_idx = jnp.arange(256, dtype=jnp.int32)[:, None]
    outer_idx = jnp.arange(128, dtype=jnp.int32)[None, :]
    offset = outer_idx + 128 - inner_idx
    inside = (offset >= 0) & (offset < coeffs.shape[-1])
    picked = jnp.take(coeffs, jnp.clip(offset, 0, coeffs.shape[-1] - 1), axis=-1)
    return jnp.where(inside, picked, jnp.zeros_like(picked))

def fir_pass(signal, matrix, einsum_form):
    blocks = signal.reshape(signal.shape[:-1] + (signal.shape[-1] // 128, 128))
    joined = jnp.concatenate([jnp.roll(blocks, 1, axis=-2), blocks], axis=-1)
    result = jnp.einsum(einsum_form, joined.astype(jnp.float32), matrix.astype(jnp.float32), precision=lax.Precision.HIGHEST)
    return result.reshape(signal.shape)

def reference(raw_strain, bandpass, whiten_taps, segment_mask, channel_block, source_block):
    filtered = fir_pass(raw_strain, fir_matrix(bandpass), 'gcbi,io->gcbo')
    energy = lax.optimization_barrier(jnp.mean(filtered * filtered, axis=-1, keepdims=True))
    normalized = (filtered / jnp.sqrt(energy + 1e-05)).astype(jnp.bfloat16)
    whitened = fir_pass(normalized, fir_matrix(whiten_taps), 'gcbi,cio->gcbo').astype(jnp.bfloat16)
    bin_index = KLO + jnp.arange(FBINS, dtype=jnp.int32)
    sample_idx = jnp.arange(SAMPLES, dtype=jnp.int32)
    phase_idx = sample_idx[:, None] * bin_index[None, :] % SAMPLES
    angles = phase_idx.astype(jnp.float32) * (2.0 * math.pi / SAMPLES)
    dft_table = jnp.concatenate([jnp.cos(angles).astype(jnp.bfloat16), (-jnp.sin(angles)).astype(jnp.bfloat16)], axis=1)
    spectra = jnp.dot(whitened.reshape(-1, SAMPLES).astype(jnp.float32), dft_table.astype(jnp.float32), precision=lax.Precision.HIGHEST)
    mask_all = segment_mask.astype(jnp.float32)
    spectra = spectra.reshape(SEGS, CHANNELS, 2, FBINS) * mask_all[:, :, None, None]
    spectra = spectra.astype(jnp.bfloat16).astype(jnp.float32)
    member = channel_block == source_block[0]
    member_rank = jnp.cumsum(member.astype(jnp.int32)) - 1
    chosen = member[None, :] & (member_rank[None, :] == jnp.arange(BLOCK, dtype=jnp.int32)[:, None])
    selector = chosen.astype(jnp.float32)
    sources = jnp.einsum('sc,gckf->gskf', selector, spectra, precision=lax.Precision.HIGHEST)
    turned = jnp.stack([-sources[:, :, 1], sources[:, :, 0]], axis=2)
    paired = jnp.stack([sources, turned], axis=0)
    stacked = jnp.einsum('jgskf,grkf->srjf', paired, spectra, precision=lax.Precision.HIGHEST)
    stacked = stacked.astype(jnp.bfloat16)
    source_mask = jnp.dot(mask_all, selector.T, precision=lax.Precision.HIGHEST)
    counts = jnp.dot(source_mask.T, mask_all, precision=lax.Precision.HIGHEST)
    lag_index = jnp.arange(LAGS, dtype=jnp.int32) - LAGS // 2
    lag_phase = bin_index[:, None] * lag_index[None, :] % SAMPLES
    lag_angles = lag_phase.astype(jnp.float32) * (2.0 * math.pi / SAMPLES)
    lag_table = jnp.concatenate([jnp.cos(lag_angles).astype(jnp.bfloat16), (-jnp.sin(lag_angles)).astype(jnp.bfloat16)], axis=0)
    lagged = jnp.dot(stacked.reshape(BLOCK * CHANNELS, 2 * FBINS).astype(jnp.float32), lag_table.astype(jnp.float32), precision=lax.Precision.HIGHEST)
    lagged = lagged.reshape(BLOCK, CHANNELS, LAGS)
    factor = 2.0 / (SAMPLES * math.sqrt(FBINS))
    return (lagged * factor / jnp.maximum(counts, 1.0)[:, :, None]).astype(jnp.bfloat16)
```

```python
import functools
import math

import jax
import numpy as np
import jax.numpy as jnp
from jax import lax
from jax.experimental import pallas as pl
from jax.experimental.pallas import tpu as pltpu
from jax.sharding import PartitionSpec as P

SAMPLES = 4096
KLO = 64
FBINS = 512
LAGS = 1024
BLOCK = 128
GROUP = 16
GROUPS = FBINS // GROUP
PIECES = 4
CROSS = 1
BATCH = 4
PIECE_KEY, HOP_KEY = 2, 2


def table(phase):
    angles = phase.astype(np.float32) * np.float32(2.0 * math.pi / SAMPLES)
    return np.cos(angles).astype(jnp.bfloat16), (-np.sin(angles)).astype(jnp.bfloat16)


def bin_order():
    bins = KLO + np.arange(FBINS)
    return np.concatenate([bins[bins % 2 == 0], bins[bins % 2 == 1]])


def dft_table():
    time = np.arange(SAMPLES // 2)[:, None]
    parts = [np.concatenate(table(time * bins[None, :] % SAMPLES), axis=1) for bins in np.split(bin_order(), 4)]
    return np.stack(parts)


def lag_table_np():
    bins = bin_order().reshape(GROUPS, GROUP)
    lags = (np.arange(LAGS) - LAGS // 2)[None, :]
    return np.concatenate([part for group in bins for part in table(group[:, None] * lags % SAMPLES)], axis=0)


def toeplitz(taps):
    turned = pltpu.roll(jnp.broadcast_to(taps, (128, 128)), 0, 1, stride=1, stride_axis=0)
    row = lax.broadcasted_iota(jnp.int32, (128, 128), 0)
    lane = lax.broadcasted_iota(jnp.int32, (128, 128), 1)
    before = jnp.where(lane < row, turned, 0.0)
    here = jnp.where(lane >= row, turned, 0.0)
    return jnp.concatenate([before, here], axis=0).astype(jnp.bfloat16)


def exchange(parts):
    parts = list(parts)
    lane = lax.broadcasted_iota(jnp.int32, parts[0].shape, 1)
    if parts[0].dtype == jnp.bfloat16:
        lane = lane.astype(jnp.int16)
    bit = len(parts) // 2
    while bit:
        width = bit * 128 // len(parts)
        upper = (lane & width) != 0
        for i in range(len(parts)):
            if i & bit:
                continue
            a, b = parts[i], parts[i | bit]
            parts[i] = jnp.where(upper, pltpu.roll(b, width, 1), a)
            parts[i | bit] = jnp.where(upper, b, pltpu.roll(a, 128 - width, 1))
        bit //= 2
    return parts


def iota(shape, dim):
    return lax.broadcasted_iota(jnp.int32, shape, dim)


def one_hot(condition):
    return jnp.where(condition, 1.0, 0.0).astype(jnp.bfloat16)


def dot(a, b):
    return jnp.dot(a, b, preferred_element_type=jnp.float32)


def dot_nt(a, b):
    return lax.dot_general(a, b, (((1,), (1,)), ((), ())), preferred_element_type=jnp.float32)


def main_kernel(
    count, raw_hbm, band_hbm, taps_hbm, mask_hbm, block_hbm, source_ref, table_hbm, out_hbm,
    band_ref, taps_ref, mask_ref, block_ref, raw_ref, table_ref, filt, inv, white, acc, gath, loc, bd, sel, scale, scr,
    out_ref, load_sem, out_sem, near_sem, far_sem, recv_sem, core_sem,
):
    segs, rows, samples = raw_ref.shape
    levels = count // 4
    channels = count * rows
    width = rows * 2 * GROUP
    per_piece = GROUPS // PIECES
    me = lax.axis_index("chan")
    level, side, core = me // 4, (me // 2) % 2, me % 2
    y_peer = me + 2 - 4 * side
    core_peer = me + 1 - 2 * core
    has_up, has_down = level < levels - 1, level > 0
    barrier = pltpu.get_barrier_semaphore()

    small_loads = [
        pltpu.make_async_copy(far, near, load_sem.at[5 + k])
        for k, (far, near) in enumerate(
            ((block_hbm, block_ref), (mask_hbm, mask_ref), (band_hbm, band_ref), (taps_hbm, taps_ref))
        )
    ]
    for load in small_loads:
        load.start()
    raw_load = pltpu.make_async_copy(raw_hbm, raw_ref, load_sem.at[0])
    raw_load.start()
    table_loads = [
        pltpu.make_async_copy(table_hbm.at[b], table_ref.at[b], load_sem.at[1 + b]) for b in range(4)
    ]
    for load in table_loads:
        load.start()

    def greet(peer):
        pl.semaphore_signal(barrier, inc=1, device_id={"chan": peer}, device_id_type=pl.DeviceIdType.MESH)

    greet(y_peer)
    greet(core_peer)

    @pl.when(has_up)
    def _():
        greet(me + 4)

    @pl.when(has_down)
    def _():
        greet(me - 4)

    for load in small_loads:
        load.wait()
    member = block_ref[...] == source_ref[0]
    before = one_hot(iota((channels, channels), 0) < iota((channels, channels), 1))
    rank = dot(jnp.broadcast_to(one_hot(member), (8, channels)), before)[:1]
    chosen = member & (rank.astype(jnp.int32) == iota((BLOCK, channels), 0))
    picks = one_hot(chosen)
    sel[...] = picks
    mask = mask_ref[...].astype(jnp.float32).astype(jnp.bfloat16)
    spread = one_hot(iota((channels, width), 0) == me * rows + iota((channels, width), 1) // (2 * GROUP))
    mask_rows = dot(mask, spread)
    source_mask = dot_nt(picks, mask).astype(jnp.bfloat16)
    counts = dot(source_mask, mask_rows.astype(jnp.bfloat16))
    scale[...] = (2.0 / (SAMPLES * math.sqrt(FBINS))) / jnp.maximum(counts, 1.0)
    here = one_hot(iota((rows, channels), 1) == me * rows + iota((rows, channels), 0))
    mask_here = dot_nt(here, mask).astype(jnp.bfloat16)
    mask_segs = dot(mask_here, one_hot(iota((segs, 128), 0) == iota((segs, 128), 1) // GROUP))

    widen = lambda x: jnp.pad(x.astype(jnp.float32), ((0, 0), (0, 128 - x.shape[1])))
    matrix = toeplitz(widen(band_ref[...]))
    taps = widen(taps_ref[...])
    blocks = samples // 128
    raw_load.wait()
    power = jnp.zeros((segs * rows, 128), jnp.float32)
    for b in range(blocks):
        if b == 0:
            joined = jnp.concatenate([raw_ref[:, :, samples - 128 :], raw_ref[:, :, :128]], axis=2)
        else:
            joined = raw_ref[:, :, (b - 1) * 128 : (b + 1) * 128]
        part = dot(joined.reshape(segs * rows, 256), matrix)
        power = power + part * part
        filt[:, :, b * 128 : (b + 1) * 128] = part.reshape(segs, rows, 128)
    energy = jnp.sum(power, axis=1, keepdims=True) * (1.0 / samples)
    inv[...] = jnp.broadcast_to(1.0 / jnp.sqrt(energy + 1e-05), (segs * rows, 128)).reshape(segs, rows, 128)
    for c in range(rows):
        matrix = toeplitz(taps[c : c + 1, :])
        gain = inv[:, c, :]
        now = jnp.concatenate([filt[:, c, b * 128 : (b + 1) * 128] * gain for b in range(blocks)], axis=0)
        past = jnp.concatenate([now[-segs:], now[:-segs]], axis=0)
        part = dot(jnp.concatenate([past, now], axis=1).astype(jnp.bfloat16), matrix)
        for b in range(blocks):
            white[c * segs : (c + 1) * segs, b * 128 : (b + 1) * 128] = part[b * segs : (b + 1) * segs]

    pl.semaphore_wait(barrier, 2 + has_up.astype(jnp.int32) + has_down.astype(jnp.int32))

    def place(block, piece, blocks=1):
        first = block * rows if isinstance(block, int) else pl.multiple_of(block * rows, rows)
        return gath.at[piece, pl.ds(first, blocks * rows)]

    def copy(block, piece, sent, got, peer, blocks=1):
        return pltpu.make_async_remote_copy(
            src_ref=place(block, piece, blocks),
            dst_ref=place(block, piece, blocks),
            send_sem=sent.at[piece],
            recv_sem=got,
            device_id={"chan": peer},
            device_id_type=pl.DeviceIdType.MESH,
        )

    def to_core(block, piece):
        copy(block, piece, near_sem, core_sem.at[piece], core_peer).start()

    def to_y(far, piece):
        copy(far * 4 + side * 2 + core, piece, near_sem, recv_sem.at[far * 2 + 1, piece], y_peer).start()

    def to_z(far, other, piece, up):
        block = far * 4 + (1 - side if other else side) * 2 + core

        @pl.when(has_up if up else has_down)
        def _():
            copy(block, piece, far_sem, recv_sem.at[far * 2 + other, piece], me + 4 if up else me - 4).start()

    def arrived(far, other, piece):
        copy(me, piece, near_sem, recv_sem.at[far * 2 + other, piece], y_peer).wait_recv()

    def send_own(piece):
        to_z(level, 0, piece, True)
        to_z(level, 0, piece, False)
        to_y(level, piece)
        to_core(me, piece)

    def along(far, way, piece):
        arrived(far, 0, piece)
        to_z(far, 0, piece, way < 0)
        if piece >= CROSS:
            to_y(far, piece)
        to_core(far * 4 + side * 2 + core, piece)

    def across(far, way, piece):
        arrived(far, 1, piece)
        if piece < CROSS:
            if way >= 0:
                to_z(far, 1, piece, False)
            if way <= 0:
                to_z(far, 1, piece, True)
        to_core(far * 4 + (1 - side) * 2 + core, piece)

    def each(distance, piece, act):
        if distance == 0:
            act(level, 0, piece)
            return
        for way in (1, -1):
            far = level + way * distance

            @pl.when((far >= 0) & (far < levels))
            def _():
                act(far, way, piece)

    half = samples // 2
    mine = pl.ds(pl.multiple_of(me * rows, rows), rows)
    for b in range(4):
        if b % 2 == 0:
            early = white[:, :half].astype(jnp.bfloat16).astype(jnp.float32)
            late = white[:, half:].astype(jnp.bfloat16).astype(jnp.float32)
            folded = (early + late if b == 0 else early - late).astype(jnp.bfloat16)
        table_loads[b].wait()
        spectra = dot(folded, table_ref[b])
        for part in range(2):
            acc[b, part] = spectra[:, part * 128 : (part + 1) * 128]
            for k, value in enumerate(exchange([acc[b, part, pl.ds(g, rows, stride=segs), :] for g in range(segs)])):
                group = 8 * b + k
                first = group % per_piece * 256 + part * 128
                gath[group // per_piece, mine, first : first + 128] = (value * mask_segs).astype(jnp.bfloat16)
        for piece in range(b * PIECES // 4, (b + 1) * PIECES // 4):
            send_own(piece)

    for b in range(4):
        for tile in range(width // 128):
            own = [
                [acc[b, part, r * segs : (r + 1) * segs, :] for part in range(2)] for r in range(tile * 4, tile * 4 + 4)
            ]
            lanes = slice(tile * 128, (tile + 1) * 128)
            for kind, parts in enumerate(([x for re, im in own for x in (re, im)], [x for re, im in own for x in (im, -re)])):
                for k, value in enumerate(exchange(parts)):
                    loc[b * 8 + k, kind, :, lanes] = value * mask_rows[:, lanes]

    def build(group, carry):
        same = iota((GROUP, width), 0) == iota((GROUP, width), 1) % GROUP
        for kind in range(2):
            for g in range(segs):
                value = jnp.where(same, jnp.broadcast_to(loc[group, kind, g : g + 1, :], (GROUP, width)), 0.0)
                first = (kind * segs + g) * GROUP
                bd[group, first : first + GROUP, :] = value.astype(jnp.bfloat16)
        return carry

    lax.fori_loop(0, GROUPS, build, 0)

    def store(batch):
        return pltpu.make_async_copy(out_ref.at[batch], out_hbm.at[batch], out_sem.at[batch])

    def compute(piece):
        copy(0, piece, near_sem, core_sem.at[piece], core_peer, 2 * levels).wait_recv()

        def batch(index, carry):
            lanes = pl.ds(pl.multiple_of(index * BATCH * 256, BATCH * 256), BATCH * 256)
            sources = dot(sel[...], gath[piece, :, lanes]).astype(jnp.bfloat16)
            here = piece * (per_piece // BATCH) + index
            crossed = [dot(sources[:, k * 256 : (k + 1) * 256], bd[here * BATCH + k]) for k in range(BATCH)]
            for tile in range(width // 128):
                lanes = slice(tile * 128, (tile + 1) * 128)
                parts = exchange([(value[:, lanes] * scale[:, lanes]).astype(jnp.bfloat16) for value in crossed])
                for k, value in enumerate(parts):
                    scr[pl.ds(tile * 4 + k, BLOCK, stride=rows), :] = value.astype(jnp.float32)
            out_ref[here] = scr[...].astype(jnp.bfloat16)
            store(here).start()
            return carry

        lax.fori_loop(0, per_piece // BATCH, batch, 0)

    events = []
    for piece in range(PIECES):
        for distance in range(levels):
            if distance:
                events.append((piece * PIECE_KEY + distance * HOP_KEY, piece, distance, along))
            events.append((piece * PIECE_KEY + (distance + 1) * HOP_KEY, piece, distance, across))
        events.append((piece * PIECE_KEY + (levels + 1) * HOP_KEY, piece, -1, None))
    for _, piece, distance, act in sorted(events, key=lambda event: event[:3]):
        if act is None:
            compute(piece)
        else:
            each(distance, piece, act)

    for piece in range(PIECES):
        crossing = piece < CROSS
        copy(0, piece, near_sem, core_sem.at[piece], core_peer, 2 * levels + (1 if crossing else levels)).wait_send()
        each_way = 2 if crossing else 1

        @pl.when(has_up & has_down)
        def _():
            copy(0, piece, far_sem, core_sem.at[piece], core_peer, each_way * (levels + 1)).wait_send()

        @pl.when(has_up != has_down)
        def _():
            copy(0, piece, far_sem, core_sem.at[piece], core_peer, each_way).wait_send()

    for batch in range(GROUPS // BATCH):
        store(batch).wait()


def main(count, raw, bandpass, whiten_taps, segment_mask, channel_block, source_block):
    segs, rows, samples = raw.shape
    channels = count * rows
    hbm = pl.BlockSpec(memory_space=pltpu.HBM)
    return pl.pallas_call(
        functools.partial(main_kernel, count),
        out_shape=jax.ShapeDtypeStruct((GROUPS // BATCH, BLOCK * rows, 128), jnp.bfloat16),
        in_specs=[hbm, hbm, hbm, hbm, hbm, pl.BlockSpec(memory_space=pltpu.SMEM), hbm],
        out_specs=hbm,
        scratch_shapes=[
            pltpu.VMEM((1, bandpass.shape[0]), bandpass.dtype),
            pltpu.VMEM(whiten_taps.shape, whiten_taps.dtype),
            pltpu.VMEM(segment_mask.shape, segment_mask.dtype),
            pltpu.VMEM((1, channels), channel_block.dtype),
            pltpu.VMEM((segs, rows, samples), jnp.bfloat16),
            pltpu.VMEM((4, samples // 2, 256), jnp.bfloat16),
            pltpu.VMEM((segs, rows, samples), jnp.float32),
            pltpu.VMEM((segs, rows, 128), jnp.float32),
            pltpu.VMEM((rows * segs, samples), jnp.float32),
            pltpu.VMEM((4, 2, rows * segs, 128), jnp.float32),
            pltpu.VMEM((PIECES, channels, GROUPS // PIECES * 256), jnp.bfloat16),
            pltpu.VMEM((GROUPS, 2, segs, 2 * rows * GROUP), jnp.float32),
            pltpu.VMEM((GROUPS, 256, 2 * rows * GROUP), jnp.bfloat16),
            pltpu.VMEM((BLOCK, channels), jnp.bfloat16),
            pltpu.VMEM((BLOCK, 2 * rows * GROUP), jnp.float32),
            pltpu.VMEM((BLOCK * rows, 128), jnp.float32),
            pltpu.VMEM((GROUPS // BATCH, BLOCK * rows, 128), jnp.bfloat16),
            pltpu.SemaphoreType.DMA((9,)),
            pltpu.SemaphoreType.DMA((GROUPS // BATCH,)),
            pltpu.SemaphoreType.DMA((PIECES,)),
            pltpu.SemaphoreType.DMA((PIECES,)),
            pltpu.SemaphoreType.DMA((count // 2, PIECES)),
            pltpu.SemaphoreType.DMA((PIECES,)),
        ],
        compiler_params=pltpu.CompilerParams(
            collective_id=0, has_side_effects=True, vmem_limit_bytes=56 * 2**20
        ),
    )(raw, bandpass[None], whiten_taps, segment_mask, channel_block[None], source_block, jnp.asarray(dft_table()))


STEPS = 4


def lag_kernel(stacked_ref, lag_ref, out_ref):
    stacked = jnp.concatenate([stacked_ref[k] for k in range(stacked_ref.shape[0])], axis=1)
    lagged = dot(stacked, lag_ref[...])
    out_ref[...] = lagged.astype(jnp.bfloat16).reshape(out_ref.shape)


def lag(stacked, rows):
    return pl.pallas_call(
        lag_kernel,
        out_shape=jax.ShapeDtypeStruct((BLOCK, rows, LAGS), jnp.bfloat16),
        grid=(STEPS,),
        in_specs=[
            pl.BlockSpec((stacked.shape[0], BLOCK // STEPS * rows, 128), lambda i: (0, i, 0)),
            pl.BlockSpec(memory_space=pltpu.VMEM),
        ],
        out_specs=pl.BlockSpec((BLOCK // STEPS, rows, LAGS), lambda i: (i, 0, 0)),
        compiler_params=pltpu.CompilerParams(vmem_limit_bytes=58 * 2**20),
        cost_estimate=pl.CostEstimate(flops=4 * 10**9, bytes_accessed=10**7, transcendentals=0),
    )(stacked, jnp.asarray(lag_table_np()))


def body(count, raw_strain, bandpass, whiten_taps, segment_mask, channel_block, source_block):
    stacked = main(count, raw_strain, bandpass, whiten_taps, segment_mask, channel_block, source_block)
    return lag(stacked, raw_strain.shape[1])


def solution(mesh):
    in_specs = (
        P(None, ("groups", "chan"), None),
        P(),
        P(("groups", "chan"), None),
        P(None, "groups"),
        P("groups"),
        P("groups"),
    )
    out_specs = P(None, ("groups", "chan"), None)
    return jax.shard_map(functools.partial(body, mesh.shape["chan"]), mesh=mesh, in_specs=in_specs, out_specs=out_specs, check_vma=False)
```

```python
import functools
import math

import jax
import numpy as np
import jax.numpy as jnp
from jax import lax
from jax.experimental import pallas as pl
from jax.experimental.pallas import tpu as pltpu
from jax.sharding import PartitionSpec as P

SAMPLES = 4096
KLO = 64
FBINS = 512
LAGS = 1024
BLOCK = 128
GROUP = 16
GROUPS = FBINS // GROUP
PIECES = 8
CROSS = 1
BATCH = 4
PIECE_KEY, HOP_KEY, COMPUTE_KEY = 1, 10, 1.5


def table(phase):
    angles = phase.astype(np.float32) * np.float32(2.0 * math.pi / SAMPLES)
    return np.cos(angles).astype(jnp.bfloat16), (-np.sin(angles)).astype(jnp.bfloat16)


def bin_order():
    bins = KLO + np.arange(FBINS)
    return np.concatenate([bins[bins % 2 == 0], bins[bins % 2 == 1]])


def dft_table():
    time = np.arange(SAMPLES // 2)[:, None]
    parts = [np.concatenate(table(time * bins[None, :] % SAMPLES), axis=1) for bins in np.split(bin_order(), 4)]
    return np.stack(parts)


def lag_table_np():
    bins = bin_order().reshape(GROUPS, GROUP)
    lags = (np.arange(LAGS) - LAGS // 2)[None, :]
    return np.concatenate([part for group in bins for part in table(group[:, None] * lags % SAMPLES)], axis=0)


def toeplitz(taps):
    turned = pltpu.roll(jnp.broadcast_to(taps, (128, 128)), 0, 1, stride=1, stride_axis=0)
    row = lax.broadcasted_iota(jnp.int32, (128, 128), 0)
    lane = lax.broadcasted_iota(jnp.int32, (128, 128), 1)
    before = jnp.where(lane < row, turned, 0.0)
    here = jnp.where(lane >= row, turned, 0.0)
    return jnp.concatenate([before, here], axis=0).astype(jnp.bfloat16)


def exchange(parts):
    parts = list(parts)
    lane = lax.broadcasted_iota(jnp.int32, parts[0].shape, 1)
    if parts[0].dtype == jnp.bfloat16:
        lane = lane.astype(jnp.int16)
    bit = len(parts) // 2
    while bit:
        width = bit * 128 // len(parts)
        upper = (lane & width) != 0
        for i in range(len(parts)):
            if i & bit:
                continue
            a, b = parts[i], parts[i | bit]
            parts[i] = jnp.where(upper, pltpu.roll(b, width, 1), a)
            parts[i | bit] = jnp.where(upper, b, pltpu.roll(a, 128 - width, 1))
        bit //= 2
    return parts


def iota(shape, dim):
    return lax.broadcasted_iota(jnp.int32, shape, dim)


def one_hot(condition):
    return jnp.where(condition, 1.0, 0.0).astype(jnp.bfloat16)


def dot(a, b):
    return jnp.dot(a, b, preferred_element_type=jnp.float32)


def dot_nt(a, b):
    return lax.dot_general(a, b, (((1,), (1,)), ((), ())), preferred_element_type=jnp.float32)


def main_kernel(
    count, raw_hbm, band_hbm, taps_hbm, mask_hbm, block_hbm, source_ref, table_hbm, out_hbm,
    band_ref, taps_ref, mask_ref, block_ref, raw_ref, table_ref, filt, inv, white, acc, gath, loc, bd, sel, scale, scr,
    out_ref, load_sem, out_sem, near_sem, far_sem, recv_sem, core_sem,
):
    segs, rows, samples = raw_ref.shape
    levels = count // 4
    channels = count * rows
    width = rows * 2 * GROUP
    per_piece = GROUPS // PIECES
    me = lax.axis_index("chan")
    level, side, core = me // 4, (me // 2) % 2, me % 2
    y_peer = me + 2 - 4 * side
    core_peer = me + 1 - 2 * core
    has_up, has_down = level < levels - 1, level > 0
    barrier = pltpu.get_barrier_semaphore()

    small_loads = [
        pltpu.make_async_copy(far, near, load_sem.at[5 + k])
        for k, (far, near) in enumerate(
            ((block_hbm, block_ref), (mask_hbm, mask_ref), (band_hbm, band_ref), (taps_hbm, taps_ref))
        )
    ]
    for load in small_loads:
        load.start()
    raw_load = pltpu.make_async_copy(raw_hbm, raw_ref, load_sem.at[0])
    raw_load.start()
    table_loads = [
        pltpu.make_async_copy(table_hbm.at[b], table_ref.at[b], load_sem.at[1 + b]) for b in range(4)
    ]
    for load in table_loads:
        load.start()

    def greet(peer):
        pl.semaphore_signal(barrier, inc=1, device_id={"chan": peer}, device_id_type=pl.DeviceIdType.MESH)

    greet(y_peer)
    greet(core_peer)

    @pl.when(has_up)
    def _():
        greet(me + 4)

    @pl.when(has_down)
    def _():
        greet(me - 4)

    for load in small_loads:
        load.wait()
    member = block_ref[...] == source_ref[0]
    before = one_hot(iota((channels, channels), 0) < iota((channels, channels), 1))
    rank = dot(jnp.broadcast_to(one_hot(member), (8, channels)), before)[:1]
    chosen = member & (rank.astype(jnp.int32) == iota((BLOCK, channels), 0))
    picks = one_hot(chosen)
    sel[...] = picks
    mask = mask_ref[...].astype(jnp.float32).astype(jnp.bfloat16)
    spread = one_hot(iota((channels, width), 0) == me * rows + iota((channels, width), 1) // (2 * GROUP))
    mask_rows = dot(mask, spread)
    source_mask = dot_nt(picks, mask).astype(jnp.bfloat16)
    counts = dot(source_mask, mask_rows.astype(jnp.bfloat16))
    scale[...] = (2.0 / (SAMPLES * math.sqrt(FBINS))) / jnp.maximum(counts, 1.0)
    here = one_hot(iota((rows, channels), 1) == me * rows + iota((rows, channels), 0))
    mask_here = dot_nt(here, mask).astype(jnp.bfloat16)
    mask_segs = dot(mask_here, one_hot(iota((segs, 128), 0) == iota((segs, 128), 1) // GROUP))

    widen = lambda x: jnp.pad(x.astype(jnp.float32), ((0, 0), (0, 128 - x.shape[1])))
    matrix = toeplitz(widen(band_ref[...]))
    taps = widen(taps_ref[...])
    blocks = samples // 128
    raw_load.wait()
    power = jnp.zeros((segs * rows, 128), jnp.float32)
    for b in range(blocks):
        if b == 0:
            joined = jnp.concatenate([raw_ref[:, :, samples - 128 :], raw_ref[:, :, :128]], axis=2)
        else:
            joined = raw_ref[:, :, (b - 1) * 128 : (b + 1) * 128]
        part = dot(joined.reshape(segs * rows, 256), matrix)
        power = power + part * part
        filt[:, :, b * 128 : (b + 1) * 128] = part.reshape(segs, rows, 128)
    energy = jnp.sum(power, axis=1, keepdims=True) * (1.0 / samples)
    inv[...] = jnp.broadcast_to(1.0 / jnp.sqrt(energy + 1e-05), (segs * rows, 128)).reshape(segs, rows, 128)
    for c in range(rows):
        matrix = toeplitz(taps[c : c + 1, :])
        gain = inv[:, c, :]
        now = jnp.concatenate([filt[:, c, b * 128 : (b + 1) * 128] * gain for b in range(blocks)], axis=0)
        past = jnp.concatenate([now[-segs:], now[:-segs]], axis=0)
        part = dot(jnp.concatenate([past, now], axis=1).astype(jnp.bfloat16), matrix)
        for b in range(blocks):
            white[c * segs : (c + 1) * segs, b * 128 : (b + 1) * 128] = part[b * segs : (b + 1) * segs]

    pl.semaphore_wait(barrier, 2 + has_up.astype(jnp.int32) + has_down.astype(jnp.int32))

    def place(block, piece, blocks=1):
        first = block * rows if isinstance(block, int) else pl.multiple_of(block * rows, rows)
        return gath.at[piece, pl.ds(first, blocks * rows)]

    def copy(block, piece, sent, got, peer, blocks=1):
        return pltpu.make_async_remote_copy(
            src_ref=place(block, piece, blocks),
            dst_ref=place(block, piece, blocks),
            send_sem=sent.at[piece],
            recv_sem=got,
            device_id={"chan": peer},
            device_id_type=pl.DeviceIdType.MESH,
        )

    def to_core(block, piece):
        copy(block, piece, near_sem, core_sem.at[piece], core_peer).start()

    def to_y(far, piece):
        copy(far * 4 + side * 2 + core, piece, near_sem, recv_sem.at[far * 2 + 1, piece], y_peer).start()

    def to_z(far, other, piece, up):
        block = far * 4 + (1 - side if other else side) * 2 + core

        @pl.when(has_up if up else has_down)
        def _():
            copy(block, piece, far_sem, recv_sem.at[far * 2 + other, piece], me + 4 if up else me - 4).start()

    def arrived(far, other, piece):
        copy(me, piece, near_sem, recv_sem.at[far * 2 + other, piece], y_peer).wait_recv()

    def send_own(piece):
        to_z(level, 0, piece, True)
        to_z(level, 0, piece, False)
        to_y(level, piece)
        to_core(me, piece)

    def along(far, way, piece):
        arrived(far, 0, piece)
        to_z(far, 0, piece, way < 0)
        if piece >= CROSS:
            to_y(far, piece)
        to_core(far * 4 + side * 2 + core, piece)

    def across(far, way, piece):
        arrived(far, 1, piece)
        if piece < CROSS:
            if way >= 0:
                to_z(far, 1, piece, False)
            if way <= 0:
                to_z(far, 1, piece, True)
        to_core(far * 4 + (1 - side) * 2 + core, piece)

    def each(distance, piece, act):
        if distance == 0:
            act(level, 0, piece)
            return
        for way in (1, -1):
            far = level + way * distance

            @pl.when((far >= 0) & (far < levels))
            def _():
                act(far, way, piece)

    half = samples // 2
    mine = pl.ds(pl.multiple_of(me * rows, rows), rows)
    for b in range(4):
        if b % 2 == 0:
            early = white[:, :half].astype(jnp.bfloat16).astype(jnp.float32)
            late = white[:, half:].astype(jnp.bfloat16).astype(jnp.float32)
            folded = (early + late if b == 0 else early - late).astype(jnp.bfloat16)
        table_loads[b].wait()
        spectra = dot(folded, table_ref[b])
        for part in range(2):
            acc[b, part] = spectra[:, part * 128 : (part + 1) * 128]
            for k, value in enumerate(exchange([acc[b, part, pl.ds(g, rows, stride=segs), :] for g in range(segs)])):
                group = 8 * b + k
                first = group % per_piece * 256 + part * 128
                gath[group // per_piece, mine, first : first + 128] = (value * mask_segs).astype(jnp.bfloat16)
        for piece in range(b * PIECES // 4, (b + 1) * PIECES // 4):
            send_own(piece)

    for b in range(4):
        for tile in range(width // 128):
            own = [
                [acc[b, part, r * segs : (r + 1) * segs, :] for part in range(2)] for r in range(tile * 4, tile * 4 + 4)
            ]
            lanes = slice(tile * 128, (tile + 1) * 128)
            for kind, parts in enumerate(([x for re, im in own for x in (re, im)], [x for re, im in own for x in (im, -re)])):
                for k, value in enumerate(exchange(parts)):
                    loc[b * 8 + k, kind, :, lanes] = value * mask_rows[:, lanes]

    def build(group, carry):
        same = iota((GROUP, width), 0) == iota((GROUP, width), 1) % GROUP
        for kind in range(2):
            for g in range(segs):
                value = jnp.where(same, jnp.broadcast_to(loc[group, kind, g : g + 1, :], (GROUP, width)), 0.0)
                first = (kind * segs + g) * GROUP
                bd[group, first : first + GROUP, :] = value.astype(jnp.bfloat16)
        return carry

    lax.fori_loop(0, GROUPS, build, 0)

    def store(batch):
        return pltpu.make_async_copy(out_ref.at[batch], out_hbm.at[batch], out_sem.at[batch])

    def compute(piece):
        copy(0, piece, near_sem, core_sem.at[piece], core_peer, 2 * levels).wait_recv()

        def batch(index, carry):
            lanes = pl.ds(pl.multiple_of(index * BATCH * 256, BATCH * 256), BATCH * 256)
            sources = dot(sel[...], gath[piece, :, lanes]).astype(jnp.bfloat16)
            here = piece * (per_piece // BATCH) + index
            crossed = [dot(sources[:, k * 256 : (k + 1) * 256], bd[here * BATCH + k]) for k in range(BATCH)]
            for tile in range(width // 128):
                lanes = slice(tile * 128, (tile + 1) * 128)
                parts = exchange([(value[:, lanes] * scale[:, lanes]).astype(jnp.bfloat16) for value in crossed])
                for k, value in enumerate(parts):
                    scr[pl.ds(tile * 4 + k, BLOCK, stride=rows), :] = value.astype(jnp.float32)
            out_ref[here] = scr[...].astype(jnp.bfloat16)
            store(here).start()
            return carry

        lax.fori_loop(0, per_piece // BATCH, batch, 0)

    events = []
    for piece in range(PIECES):
        for distance in range(levels):
            if distance:
                events.append((piece * PIECE_KEY + distance * HOP_KEY, piece, distance, along))
            events.append((piece * PIECE_KEY + (distance + 1) * HOP_KEY, piece, distance, across))
        events.append((piece * PIECE_KEY + levels * HOP_KEY + COMPUTE_KEY, piece, -1, None))
    for _, piece, distance, act in sorted(events, key=lambda event: event[:3]):
        if act is None:
            compute(piece)
        else:
            each(distance, piece, act)

    for piece in range(PIECES):
        crossing = piece < CROSS
        copy(0, piece, near_sem, core_sem.at[piece], core_peer, 2 * levels + (1 if crossing else levels)).wait_send()
        each_way = 2 if crossing else 1

        @pl.when(has_up & has_down)
        def _():
            copy(0, piece, far_sem, core_sem.at[piece], core_peer, each_way * (levels + 1)).wait_send()

        @pl.when(has_up != has_down)
        def _():
            copy(0, piece, far_sem, core_sem.at[piece], core_peer, each_way).wait_send()

    for batch in range(GROUPS // BATCH):
        store(batch).wait()


def main(count, raw, bandpass, whiten_taps, segment_mask, channel_block, source_block):
    segs, rows, samples = raw.shape
    channels = count * rows
    hbm = pl.BlockSpec(memory_space=pltpu.HBM)
    return pl.pallas_call(
        functools.partial(main_kernel, count),
        out_shape=jax.ShapeDtypeStruct((GROUPS // BATCH, BLOCK * rows, 128), jnp.bfloat16),
        in_specs=[hbm, hbm, hbm, hbm, hbm, pl.BlockSpec(memory_space=pltpu.SMEM), hbm],
        out_specs=hbm,
        scratch_shapes=[
            pltpu.VMEM((1, bandpass.shape[0]), bandpass.dtype),
            pltpu.VMEM(whiten_taps.shape, whiten_taps.dtype),
            pltpu.VMEM(segment_mask.shape, segment_mask.dtype),
            pltpu.VMEM((1, channels), channel_block.dtype),
            pltpu.VMEM((segs, rows, samples), jnp.bfloat16),
            pltpu.VMEM((4, samples // 2, 256), jnp.bfloat16),
            pltpu.VMEM((segs, rows, samples), jnp.float32),
            pltpu.VMEM((segs, rows, 128), jnp.float32),
            pltpu.VMEM((rows * segs, samples), jnp.float32),
            pltpu.VMEM((4, 2, rows * segs, 128), jnp.float32),
            pltpu.VMEM((PIECES, channels, GROUPS // PIECES * 256), jnp.bfloat16),
            pltpu.VMEM((GROUPS, 2, segs, 2 * rows * GROUP), jnp.float32),
            pltpu.VMEM((GROUPS, 256, 2 * rows * GROUP), jnp.bfloat16),
            pltpu.VMEM((BLOCK, channels), jnp.bfloat16),
            pltpu.VMEM((BLOCK, 2 * rows * GROUP), jnp.float32),
            pltpu.VMEM((BLOCK * rows, 128), jnp.float32),
            pltpu.VMEM((GROUPS // BATCH, BLOCK * rows, 128), jnp.bfloat16),
            pltpu.SemaphoreType.DMA((9,)),
            pltpu.SemaphoreType.DMA((GROUPS // BATCH,)),
            pltpu.SemaphoreType.DMA((PIECES,)),
            pltpu.SemaphoreType.DMA((PIECES,)),
            pltpu.SemaphoreType.DMA((count // 2, PIECES)),
            pltpu.SemaphoreType.DMA((PIECES,)),
        ],
        compiler_params=pltpu.CompilerParams(
            collective_id=0, has_side_effects=True, vmem_limit_bytes=56 * 2**20
        ),
    )(raw, bandpass[None], whiten_taps, segment_mask, channel_block[None], source_block, jnp.asarray(dft_table()))


STEPS = 4


def lag_kernel(stacked_ref, lag_ref, out_ref):
    stacked = jnp.concatenate([stacked_ref[k] for k in range(stacked_ref.shape[0])], axis=1)
    lagged = dot(stacked, lag_ref[...])
    out_ref[...] = lagged.astype(jnp.bfloat16).reshape(out_ref.shape)


def lag(stacked, rows):
    return pl.pallas_call(
        lag_kernel,
        out_shape=jax.ShapeDtypeStruct((BLOCK, rows, LAGS), jnp.bfloat16),
        grid=(STEPS,),
        in_specs=[
            pl.BlockSpec((stacked.shape[0], BLOCK // STEPS * rows, 128), lambda i: (0, i, 0)),
            pl.BlockSpec(memory_space=pltpu.VMEM),
        ],
        out_specs=pl.BlockSpec((BLOCK // STEPS, rows, LAGS), lambda i: (i, 0, 0)),
        compiler_params=pltpu.CompilerParams(vmem_limit_bytes=50 * 2**20),
        cost_estimate=pl.CostEstimate(flops=4 * 10**9, bytes_accessed=10**7, transcendentals=0),
    )(stacked, jnp.asarray(lag_table_np()))


def body(count, raw_strain, bandpass, whiten_taps, segment_mask, channel_block, source_block):
    stacked = main(count, raw_strain, bandpass, whiten_taps, segment_mask, channel_block, source_block)
    return lag(stacked, raw_strain.shape[1])


def solution(mesh):
    in_specs = (
        P(None, ("groups", "chan"), None),
        P(),
        P(("groups", "chan"), None),
        P(None, "groups"),
        P("groups"),
        P("groups"),
    )
    out_specs = P(None, ("groups", "chan"), None)
    return jax.shard_map(functools.partial(body, mesh.shape["chan"]), mesh=mesh, in_specs=in_specs, out_specs=out_specs, check_vma=False)
```

```python
import functools
import math

import jax
import numpy as np
import jax.numpy as jnp
from jax import lax
from jax.experimental import pallas as pl
from jax.experimental.pallas import tpu as pltpu
from jax.sharding import PartitionSpec as P

SAMPLES = 4096
KLO = 64
FBINS = 512
LAGS = 1024
BLOCK = 128
GROUP = 16
GROUPS = FBINS // GROUP
PIECES = 4
CROSS = 1
TOGETHER = 1
BATCH = 4
PIECE_KEY, HOP_KEY, COMPUTE_KEY = 1, 10, 1.5


def table(phase):
    angles = phase.astype(np.float32) * np.float32(2.0 * math.pi / SAMPLES)
    return np.cos(angles).astype(jnp.bfloat16), (-np.sin(angles)).astype(jnp.bfloat16)


def bin_order():
    bins = KLO + np.arange(FBINS)
    return np.concatenate([bins[bins % 2 == 0], bins[bins % 2 == 1]])


def dft_table():
    time = np.arange(SAMPLES // 2)[:, None]
    parts = [np.concatenate(table(time * bins[None, :] % SAMPLES), axis=1) for bins in np.split(bin_order(), 4)]
    return np.stack(parts)


def lag_table_np():
    bins = bin_order().reshape(GROUPS, GROUP)
    lags = (np.arange(LAGS) - LAGS // 2)[None, :]
    return np.concatenate([part for group in bins for part in table(group[:, None] * lags % SAMPLES)], axis=0)


def toeplitz(taps):
    turned = pltpu.roll(jnp.broadcast_to(taps, (128, 128)), 0, 1, stride=1, stride_axis=0)
    row = lax.broadcasted_iota(jnp.int32, (128, 128), 0)
    lane = lax.broadcasted_iota(jnp.int32, (128, 128), 1)
    before = jnp.where(lane < row, turned, 0.0)
    here = jnp.where(lane >= row, turned, 0.0)
    return jnp.concatenate([before, here], axis=0).astype(jnp.bfloat16)


def exchange(parts):
    parts = list(parts)
    lane = lax.broadcasted_iota(jnp.int32, parts[0].shape, 1)
    if parts[0].dtype == jnp.bfloat16:
        lane = lane.astype(jnp.int16)
    bit = len(parts) // 2
    while bit:
        width = bit * 128 // len(parts)
        upper = (lane & width) != 0
        for i in range(len(parts)):
            if i & bit:
                continue
            a, b = parts[i], parts[i | bit]
            parts[i] = jnp.where(upper, pltpu.roll(b, width, 1), a)
            parts[i | bit] = jnp.where(upper, b, pltpu.roll(a, 128 - width, 1))
        bit //= 2
    return parts


def iota(shape, dim):
    return lax.broadcasted_iota(jnp.int32, shape, dim)


def one_hot(condition):
    return jnp.where(condition, 1.0, 0.0).astype(jnp.bfloat16)


def dot(a, b):
    return jnp.dot(a, b, preferred_element_type=jnp.float32)


def dot_nt(a, b):
    return lax.dot_general(a, b, (((1,), (1,)), ((), ())), preferred_element_type=jnp.float32)


def main_kernel(
    count, raw_hbm, band_hbm, taps_hbm, mask_hbm, block_hbm, source_ref, table_hbm, out_hbm,
    band_ref, taps_ref, mask_ref, block_ref, raw_ref, table_ref, filt, inv, white, acc, gath, loc, bd, sel, scale,
    out_ref, load_sem, out_sem, near_sem, far_sem, recv_sem, core_sem,
):
    segs, rows, samples = raw_ref.shape
    levels = count // 4
    channels = count * rows
    width = rows * 2 * GROUP
    per_piece = GROUPS // PIECES
    me = lax.axis_index("chan")
    level, side, core = me // 4, (me // 2) % 2, me % 2
    y_peer = me + 2 - 4 * side
    core_peer = me + 1 - 2 * core
    has_up, has_down = level < levels - 1, level > 0
    barrier = pltpu.get_barrier_semaphore()

    small_loads = [
        pltpu.make_async_copy(far, near, load_sem.at[5 + k])
        for k, (far, near) in enumerate(
            ((block_hbm, block_ref), (mask_hbm, mask_ref), (band_hbm, band_ref), (taps_hbm, taps_ref))
        )
    ]
    for load in small_loads:
        load.start()
    raw_load = pltpu.make_async_copy(raw_hbm, raw_ref, load_sem.at[0])
    raw_load.start()
    table_loads = [
        pltpu.make_async_copy(table_hbm.at[b], table_ref.at[b], load_sem.at[1 + b]) for b in range(4)
    ]
    for load in table_loads:
        load.start()

    def greet(peer):
        pl.semaphore_signal(barrier, inc=1, device_id={"chan": peer}, device_id_type=pl.DeviceIdType.MESH)

    greet(y_peer)
    greet(core_peer)

    @pl.when(has_up)
    def _():
        greet(me + 4)

    @pl.when(has_down)
    def _():
        greet(me - 4)

    for load in small_loads:
        load.wait()
    member = block_ref[...] == source_ref[0]
    before = one_hot(iota((channels, channels), 0) < iota((channels, channels), 1))
    rank = dot(jnp.broadcast_to(one_hot(member), (8, channels)), before)[:1]
    chosen = member & (rank.astype(jnp.int32) == iota((BLOCK, channels), 0))
    picks = one_hot(chosen)
    sel[...] = picks
    mask = mask_ref[...].astype(jnp.float32).astype(jnp.bfloat16)
    spread = one_hot(iota((channels, width), 0) == me * rows + iota((channels, width), 1) // (2 * GROUP))
    mask_rows = dot(mask, spread)
    source_mask = dot_nt(picks, mask).astype(jnp.bfloat16)
    counts = dot(source_mask, mask_rows.astype(jnp.bfloat16))
    scale[...] = (2.0 / (SAMPLES * math.sqrt(FBINS))) / jnp.maximum(counts, 1.0)
    here = one_hot(iota((rows, channels), 1) == me * rows + iota((rows, channels), 0))
    mask_here = dot_nt(here, mask).astype(jnp.bfloat16)
    mask_segs = dot(mask_here, one_hot(iota((segs, 128), 0) == iota((segs, 128), 1) // GROUP)).astype(jnp.bfloat16)

    widen = lambda x: jnp.pad(x.astype(jnp.float32), ((0, 0), (0, 128 - x.shape[1])))
    matrix = toeplitz(widen(band_ref[...]))
    taps = widen(taps_ref[...])
    blocks = samples // 128
    raw_load.wait()
    power = jnp.zeros((segs * rows, 128), jnp.float32)
    for b in range(blocks):
        if b == 0:
            joined = jnp.concatenate([raw_ref[:, :, samples - 128 :], raw_ref[:, :, :128]], axis=2)
        else:
            joined = raw_ref[:, :, (b - 1) * 128 : (b + 1) * 128]
        part = dot(joined.reshape(segs * rows, 256), matrix)
        power = power + part * part
        filt[:, :, b * 128 : (b + 1) * 128] = part.reshape(segs, rows, 128)
    energy = jnp.sum(power, axis=1, keepdims=True) * (1.0 / samples)
    inv[...] = jnp.broadcast_to(1.0 / jnp.sqrt(energy + 1e-05), (segs * rows, 128)).reshape(segs, rows, 128)
    for c in range(rows):
        matrix = toeplitz(taps[c : c + 1, :])
        gain = inv[:, c, :]
        now = jnp.concatenate([filt[:, c, b * 128 : (b + 1) * 128] * gain for b in range(blocks)], axis=0)
        past = jnp.concatenate([now[-segs:], now[:-segs]], axis=0)
        part = dot(jnp.concatenate([past, now], axis=1).astype(jnp.bfloat16), matrix)
        for b in range(blocks):
            white[c * segs : (c + 1) * segs, b * 128 : (b + 1) * 128] = part[b * segs : (b + 1) * segs]

    pl.semaphore_wait(barrier, 2 + has_up.astype(jnp.int32) + has_down.astype(jnp.int32))

    def place(block, piece, blocks=1):
        first = block * rows if isinstance(block, int) else pl.multiple_of(block * rows, rows)
        return gath.at[piece, pl.ds(first, blocks * rows)]

    def copy(block, piece, sent, got, peer, blocks=1):
        return pltpu.make_async_remote_copy(
            src_ref=place(block, piece, blocks),
            dst_ref=place(block, piece, blocks),
            send_sem=sent.at[piece],
            recv_sem=got,
            device_id={"chan": peer},
            device_id_type=pl.DeviceIdType.MESH,
        )

    def to_core(block, piece):
        copy(block, piece, near_sem, core_sem.at[piece], core_peer).start()

    def to_y(far, piece):
        copy(far * 4 + side * 2 + core, piece, near_sem, recv_sem.at[far * 2 + 1, piece], y_peer).start()

    def to_z(far, other, piece, up):
        block = far * 4 + (1 - side if other else side) * 2 + core

        @pl.when(has_up if up else has_down)
        def _():
            copy(block, piece, far_sem, recv_sem.at[far * 2 + other, piece], me + 4 if up else me - 4).start()

    def arrived(far, other, piece):
        copy(me, piece, near_sem, recv_sem.at[far * 2 + other, piece], y_peer).wait_recv()

    def send_own(piece):
        to_z(level, 0, piece, True)
        to_z(level, 0, piece, False)
        to_y(level, piece)
        to_core(me, piece)

    def along(far, way, piece):
        arrived(far, 0, piece)
        to_z(far, 0, piece, way < 0)
        if piece >= CROSS:
            to_y(far, piece)
        to_core(far * 4 + side * 2 + core, piece)

    def across(far, way, piece):
        arrived(far, 1, piece)
        if piece < CROSS:
            if way >= 0:
                to_z(far, 1, piece, False)
            if way <= 0:
                to_z(far, 1, piece, True)
        to_core(far * 4 + (1 - side) * 2 + core, piece)

    def each(distance, piece, act):
        if distance == 0:
            act(level, 0, piece)
            return
        for way in (1, -1):
            far = level + way * distance

            @pl.when((far >= 0) & (far < levels))
            def _():
                act(far, way, piece)

    half = samples // 2
    mine = pl.ds(pl.multiple_of(me * rows, rows), rows)
    for b in range(4):
        if b % 2 == 0:
            early = white[:, :half].astype(jnp.bfloat16).astype(jnp.float32)
            late = white[:, half:].astype(jnp.bfloat16).astype(jnp.float32)
            folded = (early + late if b == 0 else early - late).astype(jnp.bfloat16)
        table_loads[b].wait()
        spectra = dot(folded, table_ref[b])
        for part in range(2):
            acc[b, part] = spectra[:, part * 128 : (part + 1) * 128]
            own = [acc[b, part, pl.ds(g, rows, stride=segs), :].astype(jnp.bfloat16) for g in range(segs)]
            for k, value in enumerate(exchange(own)):
                group = 8 * b + k
                first = group % per_piece * 256 + part * 128
                gath[group // per_piece, mine, first : first + 128] = value * mask_segs
        for piece in range(b * PIECES // 4, (b + 1) * PIECES // 4):
            send_own(piece)

    for b in range(4):
        for tile in range(width // 128):
            own = [
                [acc[b, part, r * segs : (r + 1) * segs, :] for part in range(2)] for r in range(tile * 4, tile * 4 + 4)
            ]
            lanes = slice(tile * 128, (tile + 1) * 128)
            for kind, parts in enumerate(([x for re, im in own for x in (re, im)], [x for re, im in own for x in (im, -re)])):
                for k, value in enumerate(exchange(parts)):
                    loc[b * 8 + k, kind, :, lanes] = value * mask_rows[:, lanes]

    def build(group, carry):
        same = iota((GROUP, width), 0) == iota((GROUP, width), 1) % GROUP
        for kind in range(2):
            for g in range(segs):
                value = jnp.where(same, jnp.broadcast_to(loc[group, kind, g : g + 1, :], (GROUP, width)), 0.0)
                first = (kind * segs + g) * GROUP
                bd[group, first : first + GROUP, :] = value.astype(jnp.bfloat16)
        return carry

    lax.fori_loop(0, GROUPS, build, 0)

    def store(batch):
        return pltpu.make_async_copy(out_ref.at[batch], out_hbm.at[batch], out_sem.at[batch])

    def crossed(piece, batch):
        lanes = slice(batch * BATCH * 256, (batch + 1) * BATCH * 256)
        sources = dot(sel[...], gath[piece, :, lanes]).astype(jnp.bfloat16)
        first = piece * per_piece + batch * BATCH
        return [dot(sources[:, k * 256 : (k + 1) * 256], bd[first + k]) for k in range(BATCH)]

    def arrange(values, batch):
        parts = []
        for tile in range(width // 128):
            lanes = slice(tile * 128, (tile + 1) * 128)
            parts += exchange([(value[:, lanes] * scale[:, lanes]).astype(jnp.bfloat16) for value in values])
        out_ref[batch] = jnp.transpose(jnp.stack(parts), (1, 0, 2)).reshape(BLOCK * rows, 128)
        store(batch).start()

    def compute(pieces):
        for piece in pieces:
            copy(0, piece, near_sem, core_sem.at[piece], core_peer, 2 * levels).wait_recv()
        batches = [(piece, batch) for piece in pieces for batch in range(per_piece // BATCH)]
        values = [crossed(piece, batch) for piece, batch in batches]
        for (piece, batch), value in zip(batches, values):
            arrange(value, piece * (per_piece // BATCH) + batch)

    events = []
    for piece in range(PIECES):
        for distance in range(levels):
            if distance:
                events.append((piece * PIECE_KEY + distance * HOP_KEY, piece, distance, along))
            events.append((piece * PIECE_KEY + (distance + 1) * HOP_KEY, piece, distance, across))
        if piece % TOGETHER == TOGETHER - 1:
            events.append((piece * PIECE_KEY + levels * HOP_KEY + COMPUTE_KEY, piece, -1, None))
    for _, piece, distance, act in sorted(events, key=lambda event: event[:3]):
        if act is None:
            compute(range(piece + 1 - TOGETHER, piece + 1))
        else:
            each(distance, piece, act)

    for piece in range(PIECES):
        crossing = piece < CROSS
        copy(0, piece, near_sem, core_sem.at[piece], core_peer, 2 * levels + (1 if crossing else levels)).wait_send()
        each_way = 2 if crossing else 1

        @pl.when(has_up & has_down)
        def _():
            copy(0, piece, far_sem, core_sem.at[piece], core_peer, each_way * (levels + 1)).wait_send()

        @pl.when(has_up != has_down)
        def _():
            copy(0, piece, far_sem, core_sem.at[piece], core_peer, each_way).wait_send()

    for batch in range(GROUPS // BATCH):
        store(batch).wait()


def main(count, raw, bandpass, whiten_taps, segment_mask, channel_block, source_block):
    segs, rows, samples = raw.shape
    channels = count * rows
    hbm = pl.BlockSpec(memory_space=pltpu.HBM)
    return pl.pallas_call(
        functools.partial(main_kernel, count),
        out_shape=jax.ShapeDtypeStruct((GROUPS // BATCH, BLOCK * rows, 128), jnp.bfloat16),
        in_specs=[hbm, hbm, hbm, hbm, hbm, pl.BlockSpec(memory_space=pltpu.SMEM), hbm],
        out_specs=hbm,
        scratch_shapes=[
            pltpu.VMEM((1, bandpass.shape[0]), bandpass.dtype),
            pltpu.VMEM(whiten_taps.shape, whiten_taps.dtype),
            pltpu.VMEM(segment_mask.shape, segment_mask.dtype),
            pltpu.VMEM((1, channels), channel_block.dtype),
            pltpu.VMEM((segs, rows, samples), jnp.bfloat16),
            pltpu.VMEM((4, samples // 2, 256), jnp.bfloat16),
            pltpu.VMEM((segs, rows, samples), jnp.float32),
            pltpu.VMEM((segs, rows, 128), jnp.float32),
            pltpu.VMEM((rows * segs, samples), jnp.float32),
            pltpu.VMEM((4, 2, rows * segs, 128), jnp.float32),
            pltpu.VMEM((PIECES, channels, GROUPS // PIECES * 256), jnp.bfloat16),
            pltpu.VMEM((GROUPS, 2, segs, 2 * rows * GROUP), jnp.float32),
            pltpu.VMEM((GROUPS, 256, 2 * rows * GROUP), jnp.bfloat16),
            pltpu.VMEM((BLOCK, channels), jnp.bfloat16),
            pltpu.VMEM((BLOCK, 2 * rows * GROUP), jnp.float32),
            pltpu.VMEM((GROUPS // BATCH, BLOCK * rows, 128), jnp.bfloat16),
            pltpu.SemaphoreType.DMA((9,)),
            pltpu.SemaphoreType.DMA((GROUPS // BATCH,)),
            pltpu.SemaphoreType.DMA((PIECES,)),
            pltpu.SemaphoreType.DMA((PIECES,)),
            pltpu.SemaphoreType.DMA((count // 2, PIECES)),
            pltpu.SemaphoreType.DMA((PIECES,)),
        ],
        compiler_params=pltpu.CompilerParams(
            collective_id=0, has_side_effects=True, vmem_limit_bytes=56 * 2**20
        ),
    )(raw, bandpass[None], whiten_taps, segment_mask, channel_block[None], source_block, jnp.asarray(dft_table()))


STEPS = 4


def lag_kernel(stacked_ref, lag_ref, out_ref):
    stacked = jnp.concatenate([stacked_ref[k] for k in range(stacked_ref.shape[0])], axis=1)
    lagged = dot(stacked, lag_ref[...])
    out_ref[...] = lagged.astype(jnp.bfloat16).reshape(out_ref.shape)


def lag(stacked, rows):
    return pl.pallas_call(
        lag_kernel,
        out_shape=jax.ShapeDtypeStruct((BLOCK, rows, LAGS), jnp.bfloat16),
        grid=(STEPS,),
        in_specs=[
            pl.BlockSpec((stacked.shape[0], BLOCK // STEPS * rows, 128), lambda i: (0, i, 0)),
            pl.BlockSpec(memory_space=pltpu.VMEM),
        ],
        out_specs=pl.BlockSpec((BLOCK // STEPS, rows, LAGS), lambda i: (i, 0, 0)),
        compiler_params=pltpu.CompilerParams(vmem_limit_bytes=50 * 2**20),
        cost_estimate=pl.CostEstimate(flops=4 * 10**9, bytes_accessed=10**7, transcendentals=0),
    )(stacked, jnp.asarray(lag_table_np()))


def body(count, raw_strain, bandpass, whiten_taps, segment_mask, channel_block, source_block):
    stacked = main(count, raw_strain, bandpass, whiten_taps, segment_mask, channel_block, source_block)
    return lag(stacked, raw_strain.shape[1])


def solution(mesh):
    in_specs = (
        P(None, ("groups", "chan"), None),
        P(),
        P(("groups", "chan"), None),
        P(None, "groups"),
        P("groups"),
        P("groups"),
    )
    out_specs = P(None, ("groups", "chan"), None)
    return jax.shard_map(functools.partial(body, mesh.shape["chan"]), mesh=mesh, in_specs=in_specs, out_specs=out_specs, check_vma=False)
```

```python
import functools
import math

import jax
import numpy as np
import jax.numpy as jnp
from jax import lax
from jax.experimental import pallas as pl
from jax.experimental.pallas import tpu as pltpu
from jax.sharding import PartitionSpec as P

SAMPLES = 4096
KLO = 64
FBINS = 512
LAGS = 1024
BLOCK = 128
GROUP = 16
GROUPS = FBINS // GROUP
PIECES = 4
CROSS = 1
BATCH = 4
PIECE_KEY, HOP_KEY, COMPUTE_KEY = 1, 10, 1.5


def table(phase, period=SAMPLES):
    angles = phase.astype(np.float32) * np.float32(2.0 * math.pi / period)
    return np.cos(angles).astype(jnp.bfloat16), (-np.sin(angles)).astype(jnp.bfloat16)


def bin_order():
    bins = KLO + np.arange(FBINS)
    return np.concatenate([bins[bins % 2 == 0], bins[bins % 2 == 1]])


def dft_table():
    time = np.arange(SAMPLES // 2)[:, None]
    parts = [np.concatenate(table(time * bins[None, :] % SAMPLES), axis=1) for bins in np.split(bin_order(), 4)]
    return np.stack(parts)


def lag_tables():
    bins = bin_order().reshape(-1, 2, BATCH, GROUP).transpose(0, 2, 1, 3).reshape(-1, 1)
    return table(bins * (2 * np.arange(LAGS // 2) + 1)[None, :] % (2 * SAMPLES), 2 * SAMPLES)


def toeplitz(taps):
    turned = pltpu.roll(jnp.broadcast_to(taps, (128, 128)), 0, 1, stride=1, stride_axis=0)
    row = lax.broadcasted_iota(jnp.int32, (128, 128), 0)
    lane = lax.broadcasted_iota(jnp.int32, (128, 128), 1)
    before = jnp.where(lane < row, turned, 0.0)
    here = jnp.where(lane >= row, turned, 0.0)
    return jnp.concatenate([before, here], axis=0).astype(jnp.bfloat16)


def exchange(parts):
    parts = list(parts)
    lane = lax.broadcasted_iota(jnp.int32, parts[0].shape, 1)
    if parts[0].dtype == jnp.bfloat16:
        lane = lane.astype(jnp.int16)
    bit = len(parts) // 2
    while bit:
        width = bit * 128 // len(parts)
        upper = (lane & width) != 0
        for i in range(len(parts)):
            if i & bit:
                continue
            a, b = parts[i], parts[i | bit]
            parts[i] = jnp.where(upper, pltpu.roll(b, width, 1), a)
            parts[i | bit] = jnp.where(upper, b, pltpu.roll(a, 128 - width, 1))
        bit //= 2
    return parts


def iota(shape, dim):
    return lax.broadcasted_iota(jnp.int32, shape, dim)


def one_hot(condition):
    return jnp.where(condition, 1.0, 0.0).astype(jnp.bfloat16)


def dot(a, b):
    return jnp.dot(a, b, preferred_element_type=jnp.float32)


def dot_nt(a, b):
    return lax.dot_general(a, b, (((1,), (1,)), ((), ())), preferred_element_type=jnp.float32)


def main_kernel(
    count, raw_hbm, band_hbm, taps_hbm, mask_hbm, block_hbm, source_ref, table_hbm, out_hbm,
    band_ref, taps_ref, mask_ref, block_ref, raw_ref, table_ref, filt, inv, white, acc, gath, loc, bd, sel, scale,
    out_ref, load_sem, out_sem, near_sem, far_sem, recv_sem, core_sem,
):
    segs, rows, samples = raw_ref.shape
    levels = count // 4
    channels = count * rows
    width = rows * 2 * GROUP
    per_piece = GROUPS // PIECES
    me = lax.axis_index("chan")
    level, side, core = me // 4, (me // 2) % 2, me % 2
    y_peer = me + 2 - 4 * side
    core_peer = me + 1 - 2 * core
    has_up, has_down = level < levels - 1, level > 0
    barrier = pltpu.get_barrier_semaphore()

    small_loads = [
        pltpu.make_async_copy(far, near, load_sem.at[5 + k])
        for k, (far, near) in enumerate(
            ((block_hbm, block_ref), (mask_hbm, mask_ref), (band_hbm, band_ref), (taps_hbm, taps_ref))
        )
    ]
    for load in small_loads:
        load.start()
    raw_load = pltpu.make_async_copy(raw_hbm, raw_ref, load_sem.at[0])
    raw_load.start()
    table_loads = [
        pltpu.make_async_copy(table_hbm.at[b], table_ref.at[b], load_sem.at[1 + b]) for b in range(4)
    ]
    for load in table_loads:
        load.start()

    def greet(peer):
        pl.semaphore_signal(barrier, inc=1, device_id={"chan": peer}, device_id_type=pl.DeviceIdType.MESH)

    greet(y_peer)
    greet(core_peer)

    @pl.when(has_up)
    def _():
        greet(me + 4)

    @pl.when(has_down)
    def _():
        greet(me - 4)

    for load in small_loads:
        load.wait()
    member = block_ref[...] == source_ref[0]
    before = one_hot(iota((channels, channels), 0) < iota((channels, channels), 1))
    rank = dot(jnp.broadcast_to(one_hot(member), (8, channels)), before)[:1]
    chosen = member & (rank.astype(jnp.int32) == iota((BLOCK, channels), 0))
    picks = one_hot(chosen)
    sel[...] = picks
    mask = mask_ref[...].astype(jnp.float32).astype(jnp.bfloat16)
    spread = one_hot(iota((channels, width), 0) == me * rows + iota((channels, width), 1) // (2 * GROUP))
    mask_rows = dot(mask, spread)
    source_mask = dot_nt(picks, mask).astype(jnp.bfloat16)
    counts = dot(source_mask, mask_rows.astype(jnp.bfloat16))
    scale[...] = (2.0 / (SAMPLES * math.sqrt(FBINS))) / jnp.maximum(counts, 1.0)
    here = one_hot(iota((rows, channels), 1) == me * rows + iota((rows, channels), 0))
    mask_here = dot_nt(here, mask).astype(jnp.bfloat16)
    mask_segs = dot(mask_here, one_hot(iota((segs, 128), 0) == iota((segs, 128), 1) // GROUP)).astype(jnp.bfloat16)

    widen = lambda x: jnp.pad(x.astype(jnp.float32), ((0, 0), (0, 128 - x.shape[1])))
    matrix = toeplitz(widen(band_ref[...]))
    taps = widen(taps_ref[...])
    blocks = samples // 128
    raw_load.wait()
    power = jnp.zeros((segs * rows, 128), jnp.float32)
    for b in range(blocks):
        if b == 0:
            joined = jnp.concatenate([raw_ref[:, :, samples - 128 :], raw_ref[:, :, :128]], axis=2)
        else:
            joined = raw_ref[:, :, (b - 1) * 128 : (b + 1) * 128]
        part = dot(joined.reshape(segs * rows, 256), matrix)
        power = power + part * part
        filt[:, :, b * 128 : (b + 1) * 128] = part.reshape(segs, rows, 128)
    energy = jnp.sum(power, axis=1, keepdims=True) * (1.0 / samples)
    inv[...] = jnp.broadcast_to(1.0 / jnp.sqrt(energy + 1e-05), (segs * rows, 128)).reshape(segs, rows, 128)
    for c in range(rows):
        matrix = toeplitz(taps[c : c + 1, :])
        gain = inv[:, c, :]
        now = jnp.concatenate([filt[:, c, b * 128 : (b + 1) * 128] * gain for b in range(blocks)], axis=0)
        past = jnp.concatenate([now[-segs:], now[:-segs]], axis=0)
        part = dot(jnp.concatenate([past, now], axis=1).astype(jnp.bfloat16), matrix)
        for b in range(blocks):
            white[c * segs : (c + 1) * segs, b * 128 : (b + 1) * 128] = part[b * segs : (b + 1) * segs]

    pl.semaphore_wait(barrier, 2 + has_up.astype(jnp.int32) + has_down.astype(jnp.int32))

    def place(block, piece, blocks=1):
        first = block * rows if isinstance(block, int) else pl.multiple_of(block * rows, rows)
        return gath.at[piece, pl.ds(first, blocks * rows)]

    def copy(block, piece, sent, got, peer, blocks=1):
        return pltpu.make_async_remote_copy(
            src_ref=place(block, piece, blocks),
            dst_ref=place(block, piece, blocks),
            send_sem=sent.at[piece],
            recv_sem=got,
            device_id={"chan": peer},
            device_id_type=pl.DeviceIdType.MESH,
        )

    def to_core(block, piece):
        copy(block, piece, near_sem, core_sem.at[piece], core_peer).start()

    def to_y(far, piece):
        copy(far * 4 + side * 2 + core, piece, near_sem, recv_sem.at[far * 2 + 1, piece], y_peer).start()

    def to_z(far, other, piece, up):
        block = far * 4 + (1 - side if other else side) * 2 + core

        @pl.when(has_up if up else has_down)
        def _():
            copy(block, piece, far_sem, recv_sem.at[far * 2 + other, piece], me + 4 if up else me - 4).start()

    def arrived(far, other, piece):
        copy(me, piece, near_sem, recv_sem.at[far * 2 + other, piece], y_peer).wait_recv()

    def send_own(piece):
        to_z(level, 0, piece, True)
        to_z(level, 0, piece, False)
        to_y(level, piece)
        to_core(me, piece)

    def along(far, way, piece):
        arrived(far, 0, piece)
        to_z(far, 0, piece, way < 0)
        if piece >= CROSS:
            to_y(far, piece)
        to_core(far * 4 + side * 2 + core, piece)

    def across(far, way, piece):
        arrived(far, 1, piece)
        if piece < CROSS:
            if way >= 0:
                to_z(far, 1, piece, False)
            if way <= 0:
                to_z(far, 1, piece, True)
        to_core(far * 4 + (1 - side) * 2 + core, piece)

    def each(distance, piece, act):
        if distance == 0:
            act(level, 0, piece)
            return
        for way in (1, -1):
            far = level + way * distance

            @pl.when((far >= 0) & (far < levels))
            def _():
                act(far, way, piece)

    half = samples // 2
    mine = pl.ds(pl.multiple_of(me * rows, rows), rows)
    for b in range(4):
        if b % 2 == 0:
            early = white[:, :half].astype(jnp.bfloat16).astype(jnp.float32)
            late = white[:, half:].astype(jnp.bfloat16).astype(jnp.float32)
            folded = (early + late if b == 0 else early - late).astype(jnp.bfloat16)
        table_loads[b].wait()
        spectra = dot(folded, table_ref[b])
        for part in range(2):
            acc[b, part] = spectra[:, part * 128 : (part + 1) * 128]
            own = [acc[b, part, pl.ds(g, rows, stride=segs), :].astype(jnp.bfloat16) for g in range(segs)]
            for k, value in enumerate(exchange(own)):
                group = 8 * b + k
                first = group % per_piece * 256 + part * 128
                gath[group // per_piece, mine, first : first + 128] = value * mask_segs
        for piece in range(b * PIECES // 4, (b + 1) * PIECES // 4):
            send_own(piece)

    for b in range(4):
        order = 2 * (b % 2 * 128 + iota((segs, 128), 1)) + b // 2
        angle = (KLO + order).astype(jnp.float32) * (math.pi / SAMPLES)
        square = angle * angle
        cosine = 1 - square / 2 * (1 - square / 12 * (1 - square / 30 * (1 - square / 56)))
        sine = angle * (1 - square / 6 * (1 - square / 20 * (1 - square / 42 * (1 - square / 72))))
        for tile in range(width // 128):
            own = []
            for r in range(tile * 4, tile * 4 + 4):
                re, im = (
                    acc[b, part, r * segs : (r + 1) * segs, :].astype(jnp.bfloat16).astype(jnp.float32)
                    for part in range(2)
                )
                own.append((re * cosine + im * sine, im * cosine - re * sine))
            lanes = slice(tile * 128, (tile + 1) * 128)
            for kind, parts in enumerate(([x for re, im in own for x in (re, im)], [x for re, im in own for x in (im, -re)])):
                for k, value in enumerate(exchange(parts)):
                    loc[b * 8 + k, kind, :, lanes] = value * mask_rows[:, lanes]

    def build(group, carry):
        same = iota((GROUP, width), 0) == iota((GROUP, width), 1) % GROUP
        for kind in range(2):
            for g in range(segs):
                value = jnp.where(same, jnp.broadcast_to(loc[group, kind, g : g + 1, :], (GROUP, width)), 0.0)
                first = (kind * segs + g) * GROUP
                bd[group, first : first + GROUP, :] = value.astype(jnp.bfloat16)
        return carry

    lax.fori_loop(0, GROUPS, build, 0)

    def store(batch):
        return pltpu.make_async_copy(out_ref.at[batch], out_hbm.at[batch], out_sem.at[batch])

    def crossed(piece, batch):
        lanes = slice(batch * BATCH * 256, (batch + 1) * BATCH * 256)
        sources = dot(sel[...], gath[piece, :, lanes]).astype(jnp.bfloat16)
        first = piece * per_piece + batch * BATCH
        return [dot(sources[:, k * 256 : (k + 1) * 256], bd[first + k]) for k in range(BATCH)]

    def arrange(values):
        parts = []
        for tile in range(width // 128):
            lanes = slice(tile * 128, (tile + 1) * 128)
            parts += exchange([(value[:, lanes] * scale[:, lanes]).astype(jnp.bfloat16) for value in values])
        return parts

    def leave(parts, index):
        out_ref[index] = jnp.transpose(jnp.stack(parts), (1, 0, 2)).reshape(BLOCK * rows, 128)
        store(index).start()

    def compute(piece):
        copy(0, piece, near_sem, core_sem.at[piece], core_peer, 2 * levels).wait_recv()
        values = [crossed(piece, batch) for batch in range(per_piece // BATCH)]
        for pair in range(per_piece // BATCH // 2):
            first, second = (arrange(values[2 * pair + k]) for k in range(2))
            upper = (iota((BLOCK, 128), 1).astype(jnp.int16) & GROUP) != 0
            index = (piece * (per_piece // BATCH // 2) + pair) * 2
            leave([jnp.where(upper, pltpu.roll(b, GROUP, 1), a) for a, b in zip(first, second)], index)
            leave([jnp.where(upper, b, pltpu.roll(a, 128 - GROUP, 1)) for a, b in zip(first, second)], index + 1)

    events = []
    for piece in range(PIECES):
        for distance in range(levels):
            if distance:
                events.append((piece * PIECE_KEY + distance * HOP_KEY, piece, distance, along))
            events.append((piece * PIECE_KEY + (distance + 1) * HOP_KEY, piece, distance, across))
        events.append((piece * PIECE_KEY + levels * HOP_KEY + COMPUTE_KEY, piece, -1, None))
    for _, piece, distance, act in sorted(events, key=lambda event: event[:3]):
        if act is None:
            compute(piece)
        else:
            each(distance, piece, act)

    for piece in range(PIECES):
        crossing = piece < CROSS
        copy(0, piece, near_sem, core_sem.at[piece], core_peer, 2 * levels + (1 if crossing else levels)).wait_send()
        each_way = 2 if crossing else 1

        @pl.when(has_up & has_down)
        def _():
            copy(0, piece, far_sem, core_sem.at[piece], core_peer, each_way * (levels + 1)).wait_send()

        @pl.when(has_up != has_down)
        def _():
            copy(0, piece, far_sem, core_sem.at[piece], core_peer, each_way).wait_send()

    for batch in range(GROUPS // BATCH):
        store(batch).wait()


def main(count, raw, bandpass, whiten_taps, segment_mask, channel_block, source_block):
    segs, rows, samples = raw.shape
    channels = count * rows
    hbm = pl.BlockSpec(memory_space=pltpu.HBM)
    return pl.pallas_call(
        functools.partial(main_kernel, count),
        out_shape=jax.ShapeDtypeStruct((GROUPS // BATCH, BLOCK * rows, 128), jnp.bfloat16),
        in_specs=[hbm, hbm, hbm, hbm, hbm, pl.BlockSpec(memory_space=pltpu.SMEM), hbm],
        out_specs=hbm,
        scratch_shapes=[
            pltpu.VMEM((1, bandpass.shape[0]), bandpass.dtype),
            pltpu.VMEM(whiten_taps.shape, whiten_taps.dtype),
            pltpu.VMEM(segment_mask.shape, segment_mask.dtype),
            pltpu.VMEM((1, channels), channel_block.dtype),
            pltpu.VMEM((segs, rows, samples), jnp.bfloat16),
            pltpu.VMEM((4, samples // 2, 256), jnp.bfloat16),
            pltpu.VMEM((segs, rows, samples), jnp.float32),
            pltpu.VMEM((segs, rows, 128), jnp.float32),
            pltpu.VMEM((rows * segs, samples), jnp.float32),
            pltpu.VMEM((4, 2, rows * segs, 128), jnp.float32),
            pltpu.VMEM((PIECES, channels, GROUPS // PIECES * 256), jnp.bfloat16),
            pltpu.VMEM((GROUPS, 2, segs, 2 * rows * GROUP), jnp.float32),
            pltpu.VMEM((GROUPS, 256, 2 * rows * GROUP), jnp.bfloat16),
            pltpu.VMEM((BLOCK, channels), jnp.bfloat16),
            pltpu.VMEM((BLOCK, 2 * rows * GROUP), jnp.float32),
            pltpu.VMEM((GROUPS // BATCH, BLOCK * rows, 128), jnp.bfloat16),
            pltpu.SemaphoreType.DMA((9,)),
            pltpu.SemaphoreType.DMA((GROUPS // BATCH,)),
            pltpu.SemaphoreType.DMA((PIECES,)),
            pltpu.SemaphoreType.DMA((PIECES,)),
            pltpu.SemaphoreType.DMA((count // 2, PIECES)),
            pltpu.SemaphoreType.DMA((PIECES,)),
        ],
        compiler_params=pltpu.CompilerParams(
            collective_id=0, has_side_effects=True, vmem_limit_bytes=56 * 2**20
        ),
    )(raw, bandpass[None], whiten_taps, segment_mask, channel_block[None], source_block, jnp.asarray(dft_table()))


STEPS = 2


def lag_kernel(stacked_ref, cos_ref, sin_ref, out_ref):
    sources, rows, lags = out_ref.shape
    height, half = sources * rows, lags // 2
    re, im = (
        jnp.concatenate([stacked_ref[k] for k in range(part, stacked_ref.shape[0], 2)], axis=1) for part in range(2)
    )
    even, odd = dot(re, cos_ref[...]), dot(im, sin_ref[...])
    out_ref[:, :, half:] = (even + odd).astype(jnp.bfloat16).reshape(sources, rows, half)
    turned = 127 - iota((height, 128), 1)
    negative = even - odd
    for first in range(0, half, 128):
        part = jnp.take_along_axis(negative[:, first : first + 128], turned, axis=1)
        out_ref[:, :, half - first - 128 : half - first] = part.astype(jnp.bfloat16).reshape(sources, rows, 128)


def lag(stacked, rows):
    vmem = pl.BlockSpec(memory_space=pltpu.VMEM)
    return pl.pallas_call(
        lag_kernel,
        out_shape=jax.ShapeDtypeStruct((BLOCK, rows, LAGS), jnp.bfloat16),
        grid=(STEPS,),
        in_specs=[
            pl.BlockSpec((stacked.shape[0], BLOCK // STEPS * rows, 128), lambda i: (0, i, 0)),
            vmem,
            vmem,
        ],
        out_specs=pl.BlockSpec((BLOCK // STEPS, rows, LAGS), lambda i: (i, 0, 0)),
        compiler_params=pltpu.CompilerParams(vmem_limit_bytes=50 * 2**20),
        cost_estimate=pl.CostEstimate(flops=2 * 10**9, bytes_accessed=10**7, transcendentals=0),
    )(stacked, *(jnp.asarray(part) for part in lag_tables()))


def body(count, raw_strain, bandpass, whiten_taps, segment_mask, channel_block, source_block):
    stacked = main(count, raw_strain, bandpass, whiten_taps, segment_mask, channel_block, source_block)
    return lag(stacked, raw_strain.shape[1])


def solution(mesh):
    in_specs = (
        P(None, ("groups", "chan"), None),
        P(),
        P(("groups", "chan"), None),
        P(None, "groups"),
        P("groups"),
        P("groups"),
    )
    out_specs = P(None, ("groups", "chan"), None)
    return jax.shard_map(functools.partial(body, mesh.shape["chan"]), mesh=mesh, in_specs=in_specs, out_specs=out_specs, check_vma=False)
```

```python
import functools
import math

import jax
import numpy as np
import jax.numpy as jnp
from jax import lax
from jax.experimental import pallas as pl
from jax.experimental.pallas import tpu as pltpu
from jax.sharding import PartitionSpec as P

SAMPLES = 4096
KLO = 64
FBINS = 512
LAGS = 1024
BLOCK = 128
GROUP = 16
GROUPS = FBINS // GROUP
PIECES = 4
CROSS = 1
BATCH = 4
PIECE_KEY, HOP_KEY, COMPUTE_KEY = 1, 10, 1.5


def table(phase, period=SAMPLES):
    angles = phase.astype(np.float32) * np.float32(2.0 * math.pi / period)
    return np.cos(angles).astype(jnp.bfloat16), (-np.sin(angles)).astype(jnp.bfloat16)


def bin_order():
    bins = KLO + np.arange(FBINS)
    return np.concatenate([bins[bins % 2 == 0], bins[bins % 2 == 1]])


def dft_table():
    time = np.arange(SAMPLES // 2)[:, None]
    parts = [np.concatenate(table(time * bins[None, :] % SAMPLES), axis=1) for bins in np.split(bin_order(), 4)]
    return np.stack(parts)


def lag_tables():
    bins = bin_order().reshape(-1, 2, BATCH, GROUP).transpose(0, 2, 1, 3).reshape(-1, 1)
    return table(bins * (2 * np.arange(LAGS // 2) + 1)[None, :] % (2 * SAMPLES), 2 * SAMPLES)


def toeplitz(taps):
    turned = pltpu.roll(jnp.broadcast_to(taps, (128, 128)), 0, 1, stride=1, stride_axis=0)
    row = lax.broadcasted_iota(jnp.int32, (128, 128), 0)
    lane = lax.broadcasted_iota(jnp.int32, (128, 128), 1)
    before = jnp.where(lane < row, turned, 0.0)
    here = jnp.where(lane >= row, turned, 0.0)
    return jnp.concatenate([before, here], axis=0).astype(jnp.bfloat16)


def exchange(parts):
    parts = list(parts)
    lane = lax.broadcasted_iota(jnp.int32, parts[0].shape, 1)
    if parts[0].dtype == jnp.bfloat16:
        lane = lane.astype(jnp.int16)
    bit = len(parts) // 2
    while bit:
        width = bit * 128 // len(parts)
        upper = (lane & width) != 0
        for i in range(len(parts)):
            if i & bit:
                continue
            a, b = parts[i], parts[i | bit]
            parts[i] = jnp.where(upper, pltpu.roll(b, width, 1), a)
            parts[i | bit] = jnp.where(upper, b, pltpu.roll(a, 128 - width, 1))
        bit //= 2
    return parts


def iota(shape, dim):
    return lax.broadcasted_iota(jnp.int32, shape, dim)


def one_hot(condition):
    return jnp.where(condition, 1.0, 0.0).astype(jnp.bfloat16)


def dot(a, b):
    return jnp.dot(a, b, preferred_element_type=jnp.float32)


def dot_nt(a, b):
    return lax.dot_general(a, b, (((1,), (1,)), ((), ())), preferred_element_type=jnp.float32)


def main_kernel(
    count, raw_hbm, band_hbm, taps_hbm, mask_hbm, block_hbm, source_ref, table_hbm, out_hbm,
    band_ref, taps_ref, mask_ref, block_ref, raw_ref, table_ref, filt, inv, white, acc, gath, loc, bd, sel, scale,
    out_ref, load_sem, out_sem, near_sem, far_sem, recv_sem, core_sem,
):
    segs, rows, samples = raw_ref.shape
    levels = count // 4
    channels = count * rows
    width = rows * 2 * GROUP
    per_piece = GROUPS // PIECES
    me = lax.axis_index("chan")
    level, side, core = me // 4, (me // 2) % 2, me % 2
    y_peer = me + 2 - 4 * side
    core_peer = me + 1 - 2 * core
    has_up, has_down = level < levels - 1, level > 0
    barrier = pltpu.get_barrier_semaphore()

    small_loads = [
        pltpu.make_async_copy(far, near, load_sem.at[5 + k])
        for k, (far, near) in enumerate(
            ((block_hbm, block_ref), (mask_hbm, mask_ref), (band_hbm, band_ref), (taps_hbm, taps_ref))
        )
    ]
    for load in small_loads:
        load.start()
    raw_load = pltpu.make_async_copy(raw_hbm, raw_ref, load_sem.at[0])
    raw_load.start()
    table_loads = [
        pltpu.make_async_copy(table_hbm.at[b], table_ref.at[b], load_sem.at[1 + b]) for b in range(4)
    ]

    def greet(peer):
        pl.semaphore_signal(barrier, inc=1, device_id={"chan": peer}, device_id_type=pl.DeviceIdType.MESH)

    greet(y_peer)
    greet(core_peer)

    @pl.when(has_up)
    def _():
        greet(me + 4)

    @pl.when(has_down)
    def _():
        greet(me - 4)

    for load in small_loads:
        load.wait()
    member = block_ref[...] == source_ref[0]
    before = one_hot(iota((channels, channels), 0) < iota((channels, channels), 1))
    rank = dot(jnp.broadcast_to(one_hot(member), (8, channels)), before)[:1]
    chosen = member & (rank.astype(jnp.int32) == iota((BLOCK, channels), 0))
    picks = one_hot(chosen)
    sel[...] = picks
    mask = mask_ref[...].astype(jnp.float32).astype(jnp.bfloat16)
    spread = one_hot(iota((channels, width), 0) == me * rows + iota((channels, width), 1) // (2 * GROUP))
    mask_rows = dot(mask, spread)
    source_mask = dot_nt(picks, mask).astype(jnp.bfloat16)
    counts = dot(source_mask, mask_rows.astype(jnp.bfloat16))
    scale[...] = (2.0 / (SAMPLES * math.sqrt(FBINS))) / jnp.maximum(counts, 1.0)
    here = one_hot(iota((rows, channels), 1) == me * rows + iota((rows, channels), 0))
    mask_here = dot_nt(here, mask).astype(jnp.bfloat16)
    mask_segs = dot(mask_here, one_hot(iota((segs, 128), 0) == iota((segs, 128), 1) // GROUP)).astype(jnp.bfloat16)

    widen = lambda x: jnp.pad(x.astype(jnp.float32), ((0, 0), (0, 128 - x.shape[1])))
    matrix = toeplitz(widen(band_ref[...]))
    taps = widen(taps_ref[...])
    blocks = samples // 128
    raw_load.wait()
    for load in table_loads:
        load.start()
    power = jnp.zeros((segs * rows, 128), jnp.float32)
    for b in range(blocks):
        if b == 0:
            joined = jnp.concatenate([raw_ref[:, :, samples - 128 :], raw_ref[:, :, :128]], axis=2)
        else:
            joined = raw_ref[:, :, (b - 1) * 128 : (b + 1) * 128]
        part = dot(joined.reshape(segs * rows, 256), matrix)
        power = power + part * part
        filt[:, :, b * 128 : (b + 1) * 128] = part.reshape(segs, rows, 128)
    energy = jnp.sum(power, axis=1, keepdims=True) * (1.0 / samples)
    inv[...] = jnp.broadcast_to(1.0 / jnp.sqrt(energy + 1e-05), (segs * rows, 128)).reshape(segs, rows, 128)
    for c in range(rows):
        matrix = toeplitz(taps[c : c + 1, :])
        gain = inv[:, c, :]
        now = jnp.concatenate([filt[:, c, b * 128 : (b + 1) * 128] * gain for b in range(blocks)], axis=0)
        past = jnp.concatenate([now[-segs:], now[:-segs]], axis=0)
        part = dot(jnp.concatenate([past, now], axis=1).astype(jnp.bfloat16), matrix)
        for b in range(blocks):
            white[c * segs : (c + 1) * segs, b * 128 : (b + 1) * 128] = part[b * segs : (b + 1) * segs]

    pl.semaphore_wait(barrier, 2 + has_up.astype(jnp.int32) + has_down.astype(jnp.int32))

    def place(block, piece, blocks=1):
        first = block * rows if isinstance(block, int) else pl.multiple_of(block * rows, rows)
        return gath.at[piece, pl.ds(first, blocks * rows)]

    def copy(block, piece, sent, got, peer, blocks=1):
        return pltpu.make_async_remote_copy(
            src_ref=place(block, piece, blocks),
            dst_ref=place(block, piece, blocks),
            send_sem=sent.at[piece],
            recv_sem=got,
            device_id={"chan": peer},
            device_id_type=pl.DeviceIdType.MESH,
        )

    def to_core(block, piece):
        copy(block, piece, near_sem, core_sem.at[piece], core_peer).start()

    def to_y(far, piece):
        copy(far * 4 + side * 2 + core, piece, near_sem, recv_sem.at[far * 2 + 1, piece], y_peer).start()

    def to_z(far, other, piece, up):
        block = far * 4 + (1 - side if other else side) * 2 + core

        @pl.when(has_up if up else has_down)
        def _():
            copy(block, piece, far_sem, recv_sem.at[far * 2 + other, piece], me + 4 if up else me - 4).start()

    def arrived(far, other, piece):
        copy(me, piece, near_sem, recv_sem.at[far * 2 + other, piece], y_peer).wait_recv()

    def send_own(piece):
        to_z(level, 0, piece, True)
        to_z(level, 0, piece, False)
        to_y(level, piece)
        to_core(me, piece)

    def along(far, way, piece):
        arrived(far, 0, piece)
        to_z(far, 0, piece, way < 0)
        if piece < PIECES - CROSS:
            to_y(far, piece)
        to_core(far * 4 + side * 2 + core, piece)

    def across(far, way, piece):
        arrived(far, 1, piece)
        if piece >= PIECES - CROSS:
            if way >= 0:
                to_z(far, 1, piece, False)
            if way <= 0:
                to_z(far, 1, piece, True)
        to_core(far * 4 + (1 - side) * 2 + core, piece)

    def each(distance, piece, act):
        if distance == 0:
            act(level, 0, piece)
            return
        for way in (1, -1):
            far = level + way * distance

            @pl.when((far >= 0) & (far < levels))
            def _():
                act(far, way, piece)

    half = samples // 2
    mine = pl.ds(pl.multiple_of(me * rows, rows), rows)
    for b in range(4):
        if b % 2 == 0:
            early = white[:, :half].astype(jnp.bfloat16).astype(jnp.float32)
            late = white[:, half:].astype(jnp.bfloat16).astype(jnp.float32)
            folded = (early + late if b == 0 else early - late).astype(jnp.bfloat16)
        table_loads[b].wait()
        spectra = dot(folded, table_ref[b])
        for part in range(2):
            acc[b, part] = spectra[:, part * 128 : (part + 1) * 128]
            own = [acc[b, part, pl.ds(g, rows, stride=segs), :].astype(jnp.bfloat16) for g in range(segs)]
            for k, value in enumerate(exchange(own)):
                group = 8 * b + k
                first = group % per_piece * 256 + part * 128
                gath[group // per_piece, mine, first : first + 128] = value * mask_segs
        for piece in range(b * PIECES // 4, (b + 1) * PIECES // 4):
            send_own(piece)

    for b in range(4):
        order = 2 * (b % 2 * 128 + iota((segs, 128), 1)) + b // 2
        angle = (KLO + order).astype(jnp.float32) * (math.pi / SAMPLES)
        square = angle * angle
        cosine = 1 - square / 2 * (1 - square / 12 * (1 - square / 30 * (1 - square / 56)))
        sine = angle * (1 - square / 6 * (1 - square / 20 * (1 - square / 42 * (1 - square / 72))))
        for tile in range(width // 128):
            own = []
            for r in range(tile * 4, tile * 4 + 4):
                re, im = (
                    acc[b, part, r * segs : (r + 1) * segs, :].astype(jnp.bfloat16).astype(jnp.float32)
                    for part in range(2)
                )
                own.append((re * cosine + im * sine, im * cosine - re * sine))
            lanes = slice(tile * 128, (tile + 1) * 128)
            for kind, parts in enumerate(([x for re, im in own for x in (re, im)], [x for re, im in own for x in (im, -re)])):
                for k, value in enumerate(exchange(parts)):
                    loc[b * 8 + k, kind, :, lanes] = value * mask_rows[:, lanes]

    def build(group, carry):
        same = iota((GROUP, width), 0) == iota((GROUP, width), 1) % GROUP
        for kind in range(2):
            for g in range(segs):
                value = jnp.where(same, jnp.broadcast_to(loc[group, kind, g : g + 1, :], (GROUP, width)), 0.0)
                first = (kind * segs + g) * GROUP
                bd[group, first : first + GROUP, :] = value.astype(jnp.bfloat16)
        return carry

    lax.fori_loop(0, GROUPS, build, 0)

    def store(batch):
        return pltpu.make_async_copy(out_ref.at[batch], out_hbm.at[batch], out_sem.at[batch])

    def crossed(piece, batch):
        lanes = slice(batch * BATCH * 256, (batch + 1) * BATCH * 256)
        sources = dot(sel[...], gath[piece, :, lanes]).astype(jnp.bfloat16)
        first = piece * per_piece + batch * BATCH
        return [dot(sources[:, k * 256 : (k + 1) * 256], bd[first + k]) for k in range(BATCH)]

    def arrange(values):
        parts = []
        for tile in range(width // 128):
            lanes = slice(tile * 128, (tile + 1) * 128)
            parts += exchange([(value[:, lanes] * scale[:, lanes]).astype(jnp.bfloat16) for value in values])
        return parts

    def leave(parts, index):
        out_ref[index] = jnp.transpose(jnp.stack(parts), (1, 0, 2)).reshape(BLOCK * rows, 128)
        store(index).start()

    def compute(piece):
        copy(0, piece, near_sem, core_sem.at[piece], core_peer, 2 * levels).wait_recv()
        values = [crossed(piece, batch) for batch in range(per_piece // BATCH)]
        for pair in range(per_piece // BATCH // 2):
            first, second = (arrange(values[2 * pair + k]) for k in range(2))
            upper = (iota((BLOCK, 128), 1).astype(jnp.int16) & GROUP) != 0
            index = (piece * (per_piece // BATCH // 2) + pair) * 2
            leave([jnp.where(upper, pltpu.roll(b, GROUP, 1), a) for a, b in zip(first, second)], index)
            leave([jnp.where(upper, b, pltpu.roll(a, 128 - GROUP, 1)) for a, b in zip(first, second)], index + 1)

    events = []
    for piece in range(PIECES):
        for distance in range(levels):
            if distance:
                events.append((piece * PIECE_KEY + distance * HOP_KEY, piece, distance, along))
            events.append((piece * PIECE_KEY + (distance + 1) * HOP_KEY, piece, distance, across))
        events.append((piece * PIECE_KEY + levels * HOP_KEY + COMPUTE_KEY, piece, -1, None))
    for _, piece, distance, act in sorted(events, key=lambda event: event[:3]):
        if act is None:
            compute(piece)
        else:
            each(distance, piece, act)

    for piece in range(PIECES):
        crossing = piece >= PIECES - CROSS
        copy(0, piece, near_sem, core_sem.at[piece], core_peer, 2 * levels + (1 if crossing else levels)).wait_send()
        each_way = 2 if crossing else 1

        @pl.when(has_up & has_down)
        def _():
            copy(0, piece, far_sem, core_sem.at[piece], core_peer, each_way * (levels + 1)).wait_send()

        @pl.when(has_up != has_down)
        def _():
            copy(0, piece, far_sem, core_sem.at[piece], core_peer, each_way).wait_send()

    for batch in range(GROUPS // BATCH):
        store(batch).wait()


def main(count, raw, bandpass, whiten_taps, segment_mask, channel_block, source_block):
    segs, rows, samples = raw.shape
    channels = count * rows
    hbm = pl.BlockSpec(memory_space=pltpu.HBM)
    return pl.pallas_call(
        functools.partial(main_kernel, count),
        out_shape=jax.ShapeDtypeStruct((GROUPS // BATCH, BLOCK * rows, 128), jnp.bfloat16),
        in_specs=[hbm, hbm, hbm, hbm, hbm, pl.BlockSpec(memory_space=pltpu.SMEM), hbm],
        out_specs=hbm,
        scratch_shapes=[
            pltpu.VMEM((1, bandpass.shape[0]), bandpass.dtype),
            pltpu.VMEM(whiten_taps.shape, whiten_taps.dtype),
            pltpu.VMEM(segment_mask.shape, segment_mask.dtype),
            pltpu.VMEM((1, channels), channel_block.dtype),
            pltpu.VMEM((segs, rows, samples), jnp.bfloat16),
            pltpu.VMEM((4, samples // 2, 256), jnp.bfloat16),
            pltpu.VMEM((segs, rows, samples), jnp.float32),
            pltpu.VMEM((segs, rows, 128), jnp.float32),
            pltpu.VMEM((rows * segs, samples), jnp.float32),
            pltpu.VMEM((4, 2, rows * segs, 128), jnp.float32),
            pltpu.VMEM((PIECES, channels, GROUPS // PIECES * 256), jnp.bfloat16),
            pltpu.VMEM((GROUPS, 2, segs, 2 * rows * GROUP), jnp.float32),
            pltpu.VMEM((GROUPS, 256, 2 * rows * GROUP), jnp.bfloat16),
            pltpu.VMEM((BLOCK, channels), jnp.bfloat16),
            pltpu.VMEM((BLOCK, 2 * rows * GROUP), jnp.float32),
            pltpu.VMEM((GROUPS // BATCH, BLOCK * rows, 128), jnp.bfloat16),
            pltpu.SemaphoreType.DMA((9,)),
            pltpu.SemaphoreType.DMA((GROUPS // BATCH,)),
            pltpu.SemaphoreType.DMA((PIECES,)),
            pltpu.SemaphoreType.DMA((PIECES,)),
            pltpu.SemaphoreType.DMA((count // 2, PIECES)),
            pltpu.SemaphoreType.DMA((PIECES,)),
        ],
        compiler_params=pltpu.CompilerParams(
            collective_id=0, has_side_effects=True, vmem_limit_bytes=56 * 2**20
        ),
    )(raw, bandpass[None], whiten_taps, segment_mask, channel_block[None], source_block, jnp.asarray(dft_table()))


STEPS = 2


def lag_kernel(stacked_ref, cos_ref, sin_ref, out_ref):
    sources, rows, lags = out_ref.shape
    height, half = sources * rows, lags // 2
    re, im = (
        jnp.concatenate([stacked_ref[k] for k in range(part, stacked_ref.shape[0], 2)], axis=1) for part in range(2)
    )
    even, odd = dot(re, cos_ref[...]), dot(im, sin_ref[...])
    out_ref[:, :, half:] = (even + odd).astype(jnp.bfloat16).reshape(sources, rows, half)
    turned = 127 - iota((height, 128), 1)
    negative = even - odd
    for first in range(0, half, 128):
        part = jnp.take_along_axis(negative[:, first : first + 128], turned, axis=1)
        out_ref[:, :, half - first - 128 : half - first] = part.astype(jnp.bfloat16).reshape(sources, rows, 128)


def lag(stacked, rows):
    vmem = pl.BlockSpec(memory_space=pltpu.VMEM)
    return pl.pallas_call(
        lag_kernel,
        out_shape=jax.ShapeDtypeStruct((BLOCK, rows, LAGS), jnp.bfloat16),
        grid=(STEPS,),
        in_specs=[
            pl.BlockSpec((stacked.shape[0], BLOCK // STEPS * rows, 128), lambda i: (0, i, 0)),
            vmem,
            vmem,
        ],
        out_specs=pl.BlockSpec((BLOCK // STEPS, rows, LAGS), lambda i: (i, 0, 0)),
        compiler_params=pltpu.CompilerParams(vmem_limit_bytes=50 * 2**20),
        cost_estimate=pl.CostEstimate(flops=2 * 10**9, bytes_accessed=10**7, transcendentals=0),
    )(stacked, *(jnp.asarray(part) for part in lag_tables()))


def body(count, raw_strain, bandpass, whiten_taps, segment_mask, channel_block, source_block):
    stacked = main(count, raw_strain, bandpass, whiten_taps, segment_mask, channel_block, source_block)
    return lag(stacked, raw_strain.shape[1])


def solution(mesh):
    in_specs = (
        P(None, ("groups", "chan"), None),
        P(),
        P(("groups", "chan"), None),
        P(None, "groups"),
        P("groups"),
        P("groups"),
    )
    out_specs = P(None, ("groups", "chan"), None)
    return jax.shard_map(functools.partial(body, mesh.shape["chan"]), mesh=mesh, in_specs=in_specs, out_specs=out_specs, check_vma=False)
```

```python
import functools
import math

import jax
import numpy as np
import jax.numpy as jnp
from jax import lax
from jax.experimental import pallas as pl
from jax.experimental.pallas import tpu as pltpu
from jax.sharding import PartitionSpec as P

SAMPLES = 4096
KLO = 64
FBINS = 512
LAGS = 1024
BLOCK = 128
GROUP = 16
GROUPS = FBINS // GROUP
PIECES = 4
CROSS = 1
BATCH = 4
PIECE_KEY, HOP_KEY, COMPUTE_KEY = 1, 10, 1.5


def table(phase, period=SAMPLES):
    angles = phase.astype(np.float32) * np.float32(2.0 * math.pi / period)
    return np.cos(angles).astype(jnp.bfloat16), (-np.sin(angles)).astype(jnp.bfloat16)


def bin_order():
    bins = KLO + np.arange(FBINS)
    return np.concatenate([bins[bins % 2 == 0], bins[bins % 2 == 1]])


def dft_table():
    time = np.arange(SAMPLES // 2)[:, None]
    parts = [np.concatenate(table(time * bins[None, :] % SAMPLES), axis=1) for bins in np.split(bin_order(), 4)]
    return np.stack(parts)


def lag_tables():
    bins = bin_order().reshape(-1, 2, BATCH, GROUP).transpose(0, 2, 1, 3).reshape(-1, 1)
    return table(bins * (2 * np.arange(LAGS // 2) + 1)[None, :] % (2 * SAMPLES), 2 * SAMPLES)


def toeplitz(taps):
    turned = pltpu.roll(jnp.broadcast_to(taps, (128, 128)), 0, 1, stride=1, stride_axis=0)
    row = lax.broadcasted_iota(jnp.int32, (128, 128), 0)
    lane = lax.broadcasted_iota(jnp.int32, (128, 128), 1)
    before = jnp.where(lane < row, turned, 0.0)
    here = jnp.where(lane >= row, turned, 0.0)
    return jnp.concatenate([before, here], axis=0).astype(jnp.bfloat16)


def exchange(parts):
    parts = list(parts)
    lane = lax.broadcasted_iota(jnp.int32, parts[0].shape, 1)
    if parts[0].dtype == jnp.bfloat16:
        lane = lane.astype(jnp.int16)
    bit = len(parts) // 2
    while bit:
        width = bit * 128 // len(parts)
        upper = (lane & width) != 0
        for i in range(len(parts)):
            if i & bit:
                continue
            a, b = parts[i], parts[i | bit]
            parts[i] = jnp.where(upper, pltpu.roll(b, width, 1), a)
            parts[i | bit] = jnp.where(upper, b, pltpu.roll(a, 128 - width, 1))
        bit //= 2
    return parts


def iota(shape, dim):
    return lax.broadcasted_iota(jnp.int32, shape, dim)


def one_hot(condition):
    return jnp.where(condition, 1.0, 0.0).astype(jnp.bfloat16)


def dot(a, b):
    return jnp.dot(a, b, preferred_element_type=jnp.float32)


def dot_nt(a, b):
    return lax.dot_general(a, b, (((1,), (1,)), ((), ())), preferred_element_type=jnp.float32)


def main_kernel(
    count, raw_hbm, band_hbm, taps_hbm, mask_hbm, block_hbm, source_ref, table_hbm, out_hbm,
    band_ref, taps_ref, mask_ref, block_ref, raw_ref, table_ref, filt, inv, white, acc, gath, loc, bd, sel, scale,
    out_ref, load_sem, out_sem, near_sem, far_sem, recv_sem, core_sem,
):
    segs, rows, samples = raw_ref.shape
    levels = count // 4
    channels = count * rows
    width = rows * 2 * GROUP
    per_piece = GROUPS // PIECES
    me = lax.axis_index("chan")
    level, side, core = me // 4, (me // 2) % 2, me % 2
    y_peer = me + 2 - 4 * side
    core_peer = me + 1 - 2 * core
    has_up, has_down = level < levels - 1, level > 0
    barrier = pltpu.get_barrier_semaphore()

    small_loads = [
        pltpu.make_async_copy(far, near, load_sem.at[5 + k])
        for k, (far, near) in enumerate(
            ((block_hbm, block_ref), (mask_hbm, mask_ref), (band_hbm, band_ref), (taps_hbm, taps_ref))
        )
    ]
    for load in small_loads:
        load.start()
    raw_load = pltpu.make_async_copy(raw_hbm, raw_ref, load_sem.at[0])
    raw_load.start()
    table_loads = [
        pltpu.make_async_copy(table_hbm.at[b], table_ref.at[b], load_sem.at[1 + b]) for b in range(4)
    ]

    def greet(peer):
        pl.semaphore_signal(barrier, inc=1, device_id={"chan": peer}, device_id_type=pl.DeviceIdType.MESH)

    greet(y_peer)
    greet(core_peer)

    @pl.when(has_up)
    def _():
        greet(me + 4)

    @pl.when(has_down)
    def _():
        greet(me - 4)

    for load in small_loads:
        load.wait()
    member = block_ref[...] == source_ref[0]
    before = one_hot(iota((channels, channels), 0) < iota((channels, channels), 1))
    rank = dot(jnp.broadcast_to(one_hot(member), (8, channels)), before)[:1]
    chosen = member & (rank.astype(jnp.int32) == iota((BLOCK, channels), 0))
    picks = one_hot(chosen)
    sel[...] = picks
    mask = mask_ref[...].astype(jnp.float32).astype(jnp.bfloat16)
    spread = one_hot(iota((channels, width), 0) == me * rows + iota((channels, width), 1) // (2 * GROUP))
    mask_rows = dot(mask, spread)
    source_mask = dot_nt(picks, mask).astype(jnp.bfloat16)
    counts = dot(source_mask, mask_rows.astype(jnp.bfloat16))
    scale[...] = (2.0 / (SAMPLES * math.sqrt(FBINS))) / jnp.maximum(counts, 1.0)
    here = one_hot(iota((rows, channels), 1) == me * rows + iota((rows, channels), 0))
    mask_here = dot_nt(here, mask).astype(jnp.bfloat16)
    mask_segs = dot(mask_here, one_hot(iota((segs, 128), 0) == iota((segs, 128), 1) // GROUP)).astype(jnp.bfloat16)

    widen = lambda x: jnp.pad(x.astype(jnp.float32), ((0, 0), (0, 128 - x.shape[1])))
    matrix = toeplitz(widen(band_ref[...]))
    taps = widen(taps_ref[...])
    blocks = samples // 128
    raw_load.wait()
    for load in table_loads:
        load.start()
    power = jnp.zeros((segs * rows, 128), jnp.float32)
    for b in range(blocks):
        if b == 0:
            joined = jnp.concatenate([raw_ref[:, :, samples - 128 :], raw_ref[:, :, :128]], axis=2)
        else:
            joined = raw_ref[:, :, (b - 1) * 128 : (b + 1) * 128]
        part = dot(joined.reshape(segs * rows, 256), matrix)
        power = power + part * part
        filt[:, :, b * 128 : (b + 1) * 128] = part.reshape(segs, rows, 128)
    energy = jnp.sum(power, axis=1, keepdims=True) * (1.0 / samples)
    inv[...] = jnp.broadcast_to(1.0 / jnp.sqrt(energy + 1e-05), (segs * rows, 128)).reshape(segs, rows, 128)
    for c in range(rows):
        matrix = toeplitz(taps[c : c + 1, :])
        gain = inv[:, c, :]
        now = jnp.concatenate([filt[:, c, b * 128 : (b + 1) * 128] * gain for b in range(blocks)], axis=0)
        past = jnp.concatenate([now[-segs:], now[:-segs]], axis=0)
        part = dot(jnp.concatenate([past, now], axis=1).astype(jnp.bfloat16), matrix)
        for b in range(blocks):
            white[c * segs : (c + 1) * segs, b * 128 : (b + 1) * 128] = part[b * segs : (b + 1) * segs]

    pl.semaphore_wait(barrier, 2 + has_up.astype(jnp.int32) + has_down.astype(jnp.int32))

    def place(block, piece, blocks=1):
        first = block * rows if isinstance(block, int) else pl.multiple_of(block * rows, rows)
        return gath.at[piece, pl.ds(first, blocks * rows)]

    def copy(block, piece, sent, got, peer, blocks=1):
        return pltpu.make_async_remote_copy(
            src_ref=place(block, piece, blocks),
            dst_ref=place(block, piece, blocks),
            send_sem=sent.at[piece],
            recv_sem=got,
            device_id={"chan": peer},
            device_id_type=pl.DeviceIdType.MESH,
        )

    def to_core(block, piece):
        copy(block, piece, near_sem, core_sem.at[piece], core_peer).start()

    def to_y(far, piece):
        copy(far * 4 + side * 2 + core, piece, near_sem, recv_sem.at[far * 2 + 1, piece], y_peer).start()

    def to_z(far, other, piece, up):
        block = far * 4 + (1 - side if other else side) * 2 + core

        @pl.when(has_up if up else has_down)
        def _():
            copy(block, piece, far_sem, recv_sem.at[far * 2 + other, piece], me + 4 if up else me - 4).start()

    def arrived(far, other, piece):
        copy(me, piece, near_sem, recv_sem.at[far * 2 + other, piece], y_peer).wait_recv()

    def send_own(piece):
        to_z(level, 0, piece, True)
        to_z(level, 0, piece, False)
        to_y(level, piece)
        to_core(me, piece)

    def along(far, way, piece):
        arrived(far, 0, piece)
        to_z(far, 0, piece, way < 0)
        if piece < PIECES - CROSS:
            to_y(far, piece)
        to_core(far * 4 + side * 2 + core, piece)

    def across(far, way, piece):
        arrived(far, 1, piece)
        if piece >= PIECES - CROSS:
            if way >= 0:
                to_z(far, 1, piece, False)
            if way <= 0:
                to_z(far, 1, piece, True)
        to_core(far * 4 + (1 - side) * 2 + core, piece)

    def each(distance, piece, act):
        if distance == 0:
            act(level, 0, piece)
            return
        for way in (1, -1):
            far = level + way * distance

            @pl.when((far >= 0) & (far < levels))
            def _():
                act(far, way, piece)

    half = samples // 2
    mine = pl.ds(pl.multiple_of(me * rows, rows), rows)
    for b in range(4):
        if b % 2 == 0:
            early = white[:, :half].astype(jnp.bfloat16).astype(jnp.float32)
            late = white[:, half:].astype(jnp.bfloat16).astype(jnp.float32)
            folded = (early + late if b == 0 else early - late).astype(jnp.bfloat16)
        table_loads[b].wait()
        spectra = dot(folded, table_ref[b])
        for part in range(2):
            acc[b, part] = spectra[:, part * 128 : (part + 1) * 128]
            own = [acc[b, part, pl.ds(g, rows, stride=segs), :].astype(jnp.bfloat16) for g in range(segs)]
            for k, value in enumerate(exchange(own)):
                group = 8 * b + k
                first = group % per_piece * 256 + part * 128
                gath[group // per_piece, mine, first : first + 128] = value * mask_segs
        for piece in range(b * PIECES // 4, (b + 1) * PIECES // 4):
            send_own(piece)

    for b in range(4):
        order = 2 * (b % 2 * 128 + iota((segs, 128), 1)) + b // 2
        angle = (KLO + order).astype(jnp.float32) * (math.pi / SAMPLES)
        square = angle * angle
        cosine = 1 - square / 2 * (1 - square / 12 * (1 - square / 30 * (1 - square / 56)))
        sine = angle * (1 - square / 6 * (1 - square / 20 * (1 - square / 42 * (1 - square / 72))))
        for tile in range(width // 128):
            own = []
            for r in range(tile * 4, tile * 4 + 4):
                re, im = (
                    acc[b, part, r * segs : (r + 1) * segs, :].astype(jnp.bfloat16).astype(jnp.float32)
                    for part in range(2)
                )
                own.append((re * cosine + im * sine, im * cosine - re * sine))
            lanes = slice(tile * 128, (tile + 1) * 128)
            for kind, parts in enumerate(([x for re, im in own for x in (re, im)], [x for re, im in own for x in (im, -re)])):
                for k, value in enumerate(exchange(parts)):
                    loc[b * 8 + k, kind, :, lanes] = value * mask_rows[:, lanes]

    def build(group, carry):
        same = iota((GROUP, width), 0) == iota((GROUP, width), 1) % GROUP
        for kind in range(2):
            for g in range(segs):
                value = jnp.where(same, jnp.broadcast_to(loc[group, kind, g : g + 1, :], (GROUP, width)), 0.0)
                first = (kind * segs + g) * GROUP
                bd[group, first : first + GROUP, :] = value.astype(jnp.bfloat16)
        return carry

    lax.fori_loop(0, GROUPS, build, 0)

    def store(batch):
        return pltpu.make_async_copy(out_ref.at[batch], out_hbm.at[batch], out_sem.at[batch])

    def crossed(piece, batch):
        lanes = slice(batch * BATCH * 256, (batch + 1) * BATCH * 256)
        sources = dot(sel[...], gath[piece, :, lanes]).astype(jnp.bfloat16)
        first = piece * per_piece + batch * BATCH
        return [dot(sources[:, k * 256 : (k + 1) * 256], bd[first + k]) for k in range(BATCH)]

    def arrange(values):
        parts = []
        for tile in range(width // 128):
            lanes = slice(tile * 128, (tile + 1) * 128)
            parts += exchange([(value[:, lanes] * scale[:, lanes]).astype(jnp.bfloat16) for value in values])
        return parts

    def leave(parts, index):
        out_ref[index] = jnp.transpose(jnp.stack(parts), (1, 0, 2)).reshape(BLOCK * rows, 128)
        store(index).start()

    def compute(piece):
        copy(0, piece, near_sem, core_sem.at[piece], core_peer, 2 * levels).wait_recv()
        values = [crossed(piece, batch) for batch in range(per_piece // BATCH)]
        for pair in range(per_piece // BATCH // 2):
            first, second = (arrange(values[2 * pair + k]) for k in range(2))
            upper = (iota((BLOCK, 128), 1).astype(jnp.int16) & GROUP) != 0
            index = (piece * (per_piece // BATCH // 2) + pair) * 2
            leave([jnp.where(upper, pltpu.roll(b, GROUP, 1), a) for a, b in zip(first, second)], index)
            leave([jnp.where(upper, b, pltpu.roll(a, 128 - GROUP, 1)) for a, b in zip(first, second)], index + 1)

    events = []
    for piece in range(PIECES):
        for distance in range(levels):
            if distance:
                events.append((piece * PIECE_KEY + distance * HOP_KEY, piece, distance, along))
            hops = distance + 1 if piece >= PIECES - CROSS else max(distance, 2) + 1
            events.append((piece * PIECE_KEY + hops * HOP_KEY, piece, distance, across))
        events.append((piece * PIECE_KEY + levels * HOP_KEY + COMPUTE_KEY, piece, -1, None))
    for _, piece, distance, act in sorted(events, key=lambda event: event[:3]):
        if act is None:
            compute(piece)
        else:
            each(distance, piece, act)

    for piece in range(PIECES):
        crossing = piece >= PIECES - CROSS
        copy(0, piece, near_sem, core_sem.at[piece], core_peer, 2 * levels + (1 if crossing else levels)).wait_send()
        each_way = 2 if crossing else 1

        @pl.when(has_up & has_down)
        def _():
            copy(0, piece, far_sem, core_sem.at[piece], core_peer, each_way * (levels + 1)).wait_send()

        @pl.when(has_up != has_down)
        def _():
            copy(0, piece, far_sem, core_sem.at[piece], core_peer, each_way).wait_send()

    for batch in range(GROUPS // BATCH):
        store(batch).wait()


def main(count, raw, bandpass, whiten_taps, segment_mask, channel_block, source_block):
    segs, rows, samples = raw.shape
    channels = count * rows
    hbm = pl.BlockSpec(memory_space=pltpu.HBM)
    return pl.pallas_call(
        functools.partial(main_kernel, count),
        out_shape=jax.ShapeDtypeStruct((GROUPS // BATCH, BLOCK * rows, 128), jnp.bfloat16),
        in_specs=[hbm, hbm, hbm, hbm, hbm, pl.BlockSpec(memory_space=pltpu.SMEM), hbm],
        out_specs=hbm,
        scratch_shapes=[
            pltpu.VMEM((1, bandpass.shape[0]), bandpass.dtype),
            pltpu.VMEM(whiten_taps.shape, whiten_taps.dtype),
            pltpu.VMEM(segment_mask.shape, segment_mask.dtype),
            pltpu.VMEM((1, channels), channel_block.dtype),
            pltpu.VMEM((segs, rows, samples), jnp.bfloat16),
            pltpu.VMEM((4, samples // 2, 256), jnp.bfloat16),
            pltpu.VMEM((segs, rows, samples), jnp.float32),
            pltpu.VMEM((segs, rows, 128), jnp.float32),
            pltpu.VMEM((rows * segs, samples), jnp.float32),
            pltpu.VMEM((4, 2, rows * segs, 128), jnp.float32),
            pltpu.VMEM((PIECES, channels, GROUPS // PIECES * 256), jnp.bfloat16),
            pltpu.VMEM((GROUPS, 2, segs, 2 * rows * GROUP), jnp.float32),
            pltpu.VMEM((GROUPS, 256, 2 * rows * GROUP), jnp.bfloat16),
            pltpu.VMEM((BLOCK, channels), jnp.bfloat16),
            pltpu.VMEM((BLOCK, 2 * rows * GROUP), jnp.float32),
            pltpu.VMEM((GROUPS // BATCH, BLOCK * rows, 128), jnp.bfloat16),
            pltpu.SemaphoreType.DMA((9,)),
            pltpu.SemaphoreType.DMA((GROUPS // BATCH,)),
            pltpu.SemaphoreType.DMA((PIECES,)),
            pltpu.SemaphoreType.DMA((PIECES,)),
            pltpu.SemaphoreType.DMA((count // 2, PIECES)),
            pltpu.SemaphoreType.DMA((PIECES,)),
        ],
        compiler_params=pltpu.CompilerParams(
            collective_id=0, has_side_effects=True, vmem_limit_bytes=56 * 2**20
        ),
    )(raw, bandpass[None], whiten_taps, segment_mask, channel_block[None], source_block, jnp.asarray(dft_table()))


STEPS = 2


def lag_kernel(stacked_ref, cos_ref, sin_ref, out_ref):
    sources, rows, lags = out_ref.shape
    height, half = sources * rows, lags // 2
    re, im = (
        jnp.concatenate([stacked_ref[k] for k in range(part, stacked_ref.shape[0], 2)], axis=1) for part in range(2)
    )
    even, odd = dot(re, cos_ref[...]), dot(im, sin_ref[...])
    out_ref[:, :, half:] = (even + odd).astype(jnp.bfloat16).reshape(sources, rows, half)
    turned = 127 - iota((height, 128), 1)
    negative = even - odd
    for first in range(0, half, 128):
        part = jnp.take_along_axis(negative[:, first : first + 128], turned, axis=1)
        out_ref[:, :, half - first - 128 : half - first] = part.astype(jnp.bfloat16).reshape(sources, rows, 128)


def lag(stacked, rows):
    vmem = pl.BlockSpec(memory_space=pltpu.VMEM)
    return pl.pallas_call(
        lag_kernel,
        out_shape=jax.ShapeDtypeStruct((BLOCK, rows, LAGS), jnp.bfloat16),
        grid=(STEPS,),
        in_specs=[
            pl.BlockSpec((stacked.shape[0], BLOCK // STEPS * rows, 128), lambda i: (0, i, 0)),
            vmem,
            vmem,
        ],
        out_specs=pl.BlockSpec((BLOCK // STEPS, rows, LAGS), lambda i: (i, 0, 0)),
        compiler_params=pltpu.CompilerParams(vmem_limit_bytes=50 * 2**20),
        cost_estimate=pl.CostEstimate(flops=2 * 10**9, bytes_accessed=10**7, transcendentals=0),
    )(stacked, *(jnp.asarray(part) for part in lag_tables()))


def body(count, raw_strain, bandpass, whiten_taps, segment_mask, channel_block, source_block):
    stacked = main(count, raw_strain, bandpass, whiten_taps, segment_mask, channel_block, source_block)
    return lag(stacked, raw_strain.shape[1])


def solution(mesh):
    in_specs = (
        P(None, ("groups", "chan"), None),
        P(),
        P(("groups", "chan"), None),
        P(None, "groups"),
        P("groups"),
        P("groups"),
    )
    out_specs = P(None, ("groups", "chan"), None)
    return jax.shard_map(functools.partial(body, mesh.shape["chan"]), mesh=mesh, in_specs=in_specs, out_specs=out_specs, check_vma=False)
```

```python
import functools
import math

import jax
import numpy as np
import jax.numpy as jnp
from jax import lax
from jax.experimental import pallas as pl
from jax.experimental.pallas import tpu as pltpu
from jax.sharding import PartitionSpec as P

SAMPLES = 4096
KLO = 64
FBINS = 512
LAGS = 1024
BLOCK = 128
GROUP = 16
GROUPS = FBINS // GROUP
PIECES = 4
CROSS = 1
BATCH = 4
PIECE_KEY, HOP_KEY, COMPUTE_KEY = 1, 10, 1.5


def table(phase, period=SAMPLES):
    angles = phase.astype(np.float32) * np.float32(2.0 * math.pi / period)
    return np.cos(angles).astype(jnp.bfloat16), (-np.sin(angles)).astype(jnp.bfloat16)


def bin_order():
    bins = KLO + np.arange(FBINS)
    return np.concatenate([bins[bins % 2 == 0], bins[bins % 2 == 1]])


def dft_table():
    time = np.arange(SAMPLES // 2)[:, None]
    parts = [np.concatenate(table(time * bins[None, :] % SAMPLES), axis=1) for bins in np.split(bin_order(), 4)]
    return np.stack(parts)


def lag_tables():
    bins = bin_order().reshape(-1, 2, BATCH, GROUP).transpose(0, 2, 1, 3).reshape(-1, 1)
    return table(bins * (2 * np.arange(LAGS // 2) + 1)[None, :] % (2 * SAMPLES), 2 * SAMPLES)


def toeplitz(taps):
    turned = pltpu.roll(jnp.broadcast_to(taps, (128, 128)), 0, 1, stride=1, stride_axis=0)
    row = lax.broadcasted_iota(jnp.int32, (128, 128), 0)
    lane = lax.broadcasted_iota(jnp.int32, (128, 128), 1)
    before = jnp.where(lane < row, turned, 0.0)
    here = jnp.where(lane >= row, turned, 0.0)
    return jnp.concatenate([before, here], axis=0).astype(jnp.bfloat16)


def exchange(parts):
    parts = list(parts)
    lane = lax.broadcasted_iota(jnp.int32, parts[0].shape, 1)
    if parts[0].dtype == jnp.bfloat16:
        lane = lane.astype(jnp.int16)
    bit = len(parts) // 2
    while bit:
        width = bit * 128 // len(parts)
        upper = (lane & width) != 0
        for i in range(len(parts)):
            if i & bit:
                continue
            a, b = parts[i], parts[i | bit]
            parts[i] = jnp.where(upper, pltpu.roll(b, width, 1), a)
            parts[i | bit] = jnp.where(upper, b, pltpu.roll(a, 128 - width, 1))
        bit //= 2
    return parts


def iota(shape, dim):
    return lax.broadcasted_iota(jnp.int32, shape, dim)


def one_hot(condition):
    return jnp.where(condition, 1.0, 0.0).astype(jnp.bfloat16)


def dot(a, b):
    return jnp.dot(a, b, preferred_element_type=jnp.float32)


def dot_nt(a, b):
    return lax.dot_general(a, b, (((1,), (1,)), ((), ())), preferred_element_type=jnp.float32)


def main_kernel(
    count, raw_hbm, band_hbm, taps_hbm, mask_hbm, block_hbm, source_ref, table_hbm, out_hbm,
    band_ref, taps_ref, mask_ref, block_ref, raw_ref, table_ref, filt, inv, white, acc, gath, loc, bd, sel, scale,
    out_ref, load_sem, out_sem, near_sem, far_sem, recv_sem, core_sem,
):
    segs, rows, samples = raw_ref.shape
    levels = count // 4
    channels = count * rows
    width = rows * 2 * GROUP
    per_piece = GROUPS // PIECES
    me = lax.axis_index("chan")
    level, side, core = me // 4, (me // 2) % 2, me % 2
    y_peer = me + 2 - 4 * side
    core_peer = me + 1 - 2 * core
    has_up, has_down = level < levels - 1, level > 0
    barrier = pltpu.get_barrier_semaphore()

    small_loads = [
        pltpu.make_async_copy(far, near, load_sem.at[5 + k])
        for k, (far, near) in enumerate(
            ((block_hbm, block_ref), (mask_hbm, mask_ref), (band_hbm, band_ref), (taps_hbm, taps_ref))
        )
    ]
    for load in small_loads:
        load.start()
    raw_load = pltpu.make_async_copy(raw_hbm, raw_ref, load_sem.at[0])
    raw_load.start()
    table_loads = [
        pltpu.make_async_copy(table_hbm.at[b], table_ref.at[b], load_sem.at[1 + b]) for b in range(4)
    ]

    def greet(peer):
        pl.semaphore_signal(barrier, inc=1, device_id={"chan": peer}, device_id_type=pl.DeviceIdType.MESH)

    greet(y_peer)
    greet(core_peer)

    @pl.when(has_up)
    def _():
        greet(me + 4)

    @pl.when(has_down)
    def _():
        greet(me - 4)

    for load in small_loads:
        load.wait()
    member = block_ref[...] == source_ref[0]
    before = one_hot(iota((channels, channels), 0) < iota((channels, channels), 1))
    rank = dot(jnp.broadcast_to(one_hot(member), (8, channels)), before)[:1]
    chosen = member & (rank.astype(jnp.int32) == iota((BLOCK, channels), 0))
    picks = one_hot(chosen)
    sel[...] = picks
    mask = mask_ref[...].astype(jnp.float32).astype(jnp.bfloat16)
    spread = one_hot(iota((channels, width), 0) == me * rows + iota((channels, width), 1) // (2 * GROUP))
    mask_rows = dot(mask, spread)
    source_mask = dot_nt(picks, mask).astype(jnp.bfloat16)
    counts = dot(source_mask, mask_rows.astype(jnp.bfloat16))
    scale[...] = (2.0 / (SAMPLES * math.sqrt(FBINS))) / jnp.maximum(counts, 1.0)
    here = one_hot(iota((rows, channels), 1) == me * rows + iota((rows, channels), 0))
    mask_here = dot_nt(here, mask).astype(jnp.bfloat16)
    mask_segs = dot(mask_here, one_hot(iota((segs, 128), 0) == iota((segs, 128), 1) // GROUP)).astype(jnp.bfloat16)

    widen = lambda x: jnp.pad(x.astype(jnp.float32), ((0, 0), (0, 128 - x.shape[1])))
    matrix = toeplitz(widen(band_ref[...]))
    taps = widen(taps_ref[...])
    blocks = samples // 128
    raw_load.wait()
    for load in table_loads:
        load.start()
    power = jnp.zeros((segs * rows, 128), jnp.float32)
    for b in range(blocks):
        if b == 0:
            joined = jnp.concatenate([raw_ref[:, :, samples - 128 :], raw_ref[:, :, :128]], axis=2)
        else:
            joined = raw_ref[:, :, (b - 1) * 128 : (b + 1) * 128]
        part = dot(joined.reshape(segs * rows, 256), matrix)
        power = power + part * part
        filt[:, :, b * 128 : (b + 1) * 128] = part.reshape(segs, rows, 128)
    energy = jnp.sum(power, axis=1, keepdims=True) * (1.0 / samples)
    inv[...] = jnp.broadcast_to(1.0 / jnp.sqrt(energy + 1e-05), (segs * rows, 128)).reshape(segs, rows, 128)
    for c in range(rows):
        matrix = toeplitz(taps[c : c + 1, :])
        gain = inv[:, c, :]
        now = jnp.concatenate([filt[:, c, b * 128 : (b + 1) * 128] * gain for b in range(blocks)], axis=0)
        past = jnp.concatenate([now[-segs:], now[:-segs]], axis=0)
        part = dot(jnp.concatenate([past, now], axis=1).astype(jnp.bfloat16), matrix)
        for b in range(blocks):
            white[c * segs : (c + 1) * segs, b * 128 : (b + 1) * 128] = part[b * segs : (b + 1) * segs]

    pl.semaphore_wait(barrier, 2 + has_up.astype(jnp.int32) + has_down.astype(jnp.int32))

    def place(block, piece, blocks=1):
        first = block * rows if isinstance(block, int) else pl.multiple_of(block * rows, rows)
        return gath.at[piece, pl.ds(first, blocks * rows)]

    def copy(block, piece, sent, got, peer, blocks=1):
        return pltpu.make_async_remote_copy(
            src_ref=place(block, piece, blocks),
            dst_ref=place(block, piece, blocks),
            send_sem=sent.at[piece],
            recv_sem=got,
            device_id={"chan": peer},
            device_id_type=pl.DeviceIdType.MESH,
        )

    def to_core(block, piece):
        copy(block, piece, near_sem, core_sem.at[piece], core_peer).start()

    def to_y(far, piece):
        copy(far * 4 + side * 2 + core, piece, near_sem, recv_sem.at[far * 2 + 1, piece], y_peer).start()

    def to_z(far, other, piece, up):
        block = far * 4 + (1 - side if other else side) * 2 + core

        @pl.when(has_up if up else has_down)
        def _():
            copy(block, piece, far_sem, recv_sem.at[far * 2 + other, piece], me + 4 if up else me - 4).start()

    def arrived(far, other, piece):
        copy(me, piece, near_sem, recv_sem.at[far * 2 + other, piece], y_peer).wait_recv()

    def send_own(piece):
        to_core(me, piece)
        to_z(level, 0, piece, True)
        to_z(level, 0, piece, False)
        to_y(level, piece)

    def along(far, way, piece):
        arrived(far, 0, piece)
        to_core(far * 4 + side * 2 + core, piece)
        to_z(far, 0, piece, way < 0)
        if piece < PIECES - CROSS:
            to_y(far, piece)

    def across(far, way, piece):
        arrived(far, 1, piece)
        if piece >= PIECES - CROSS:
            if way >= 0:
                to_z(far, 1, piece, False)
            if way <= 0:
                to_z(far, 1, piece, True)
        to_core(far * 4 + (1 - side) * 2 + core, piece)

    def each(distance, piece, act):
        if distance == 0:
            act(level, 0, piece)
            return
        for way in (1, -1):
            far = level + way * distance

            @pl.when((far >= 0) & (far < levels))
            def _():
                act(far, way, piece)

    half = samples // 2
    mine = pl.ds(pl.multiple_of(me * rows, rows), rows)
    for b in range(4):
        if b % 2 == 0:
            early = white[:, :half].astype(jnp.bfloat16).astype(jnp.float32)
            late = white[:, half:].astype(jnp.bfloat16).astype(jnp.float32)
            folded = (early + late if b == 0 else early - late).astype(jnp.bfloat16)
        table_loads[b].wait()
        spectra = dot(folded, table_ref[b])
        for part in range(2):
            acc[b, part] = spectra[:, part * 128 : (part + 1) * 128]
            own = [acc[b, part, pl.ds(g, rows, stride=segs), :].astype(jnp.bfloat16) for g in range(segs)]
            for k, value in enumerate(exchange(own)):
                group = 8 * b + k
                first = group % per_piece * 256 + part * 128
                gath[group // per_piece, mine, first : first + 128] = value * mask_segs
        for piece in range(b * PIECES // 4, (b + 1) * PIECES // 4):
            send_own(piece)

    for b in range(4):
        order = 2 * (b % 2 * 128 + iota((segs, 128), 1)) + b // 2
        angle = (KLO + order).astype(jnp.float32) * (math.pi / SAMPLES)
        square = angle * angle
        cosine = 1 - square / 2 * (1 - square / 12 * (1 - square / 30 * (1 - square / 56)))
        sine = angle * (1 - square / 6 * (1 - square / 20 * (1 - square / 42 * (1 - square / 72))))
        for tile in range(width // 128):
            own = []
            for r in range(tile * 4, tile * 4 + 4):
                re, im = (
                    acc[b, part, r * segs : (r + 1) * segs, :].astype(jnp.bfloat16).astype(jnp.float32)
                    for part in range(2)
                )
                own.append((re * cosine + im * sine, im * cosine - re * sine))
            lanes = slice(tile * 128, (tile + 1) * 128)
            for kind, parts in enumerate(([x for re, im in own for x in (re, im)], [x for re, im in own for x in (im, -re)])):
                for k, value in enumerate(exchange(parts)):
                    loc[b * 8 + k, kind, :, lanes] = value * mask_rows[:, lanes]

    def build(group, carry):
        same = iota((GROUP, width), 0) == iota((GROUP, width), 1) % GROUP
        for kind in range(2):
            for g in range(segs):
                value = jnp.where(same, jnp.broadcast_to(loc[group, kind, g : g + 1, :], (GROUP, width)), 0.0)
                first = (kind * segs + g) * GROUP
                bd[group, first : first + GROUP, :] = value.astype(jnp.bfloat16)
        return carry

    lax.fori_loop(0, GROUPS, build, 0)

    def store(batch):
        return pltpu.make_async_copy(out_ref.at[batch], out_hbm.at[batch], out_sem.at[batch])

    def crossed(piece, batch):
        lanes = slice(batch * BATCH * 256, (batch + 1) * BATCH * 256)
        sources = dot(sel[...], gath[piece, :, lanes]).astype(jnp.bfloat16)
        first = piece * per_piece + batch * BATCH
        return [dot(sources[:, k * 256 : (k + 1) * 256], bd[first + k]) for k in range(BATCH)]

    def arrange(values):
        parts = []
        for tile in range(width // 128):
            lanes = slice(tile * 128, (tile + 1) * 128)
            parts += exchange([(value[:, lanes] * scale[:, lanes]).astype(jnp.bfloat16) for value in values])
        return parts

    def leave(parts, index):
        out_ref[index] = jnp.transpose(jnp.stack(parts), (1, 0, 2)).reshape(BLOCK * rows, 128)
        store(index).start()

    def compute(piece):
        copy(0, piece, near_sem, core_sem.at[piece], core_peer, 2 * levels).wait_recv()
        values = [crossed(piece, batch) for batch in range(per_piece // BATCH)]
        for pair in range(per_piece // BATCH // 2):
            first, second = (arrange(values[2 * pair + k]) for k in range(2))
            upper = (iota((BLOCK, 128), 1).astype(jnp.int16) & GROUP) != 0
            index = (piece * (per_piece // BATCH // 2) + pair) * 2
            leave([jnp.where(upper, pltpu.roll(b, GROUP, 1), a) for a, b in zip(first, second)], index)
            leave([jnp.where(upper, b, pltpu.roll(a, 128 - GROUP, 1)) for a, b in zip(first, second)], index + 1)

    events = []
    for piece in range(PIECES):
        for distance in range(levels):
            if distance:
                events.append((piece * PIECE_KEY + distance * HOP_KEY, piece, distance, along))
            hops = distance + 1 if piece >= PIECES - CROSS else max(distance, 2) + 1
            events.append((piece * PIECE_KEY + hops * HOP_KEY, piece, distance, across))
        events.append((piece * PIECE_KEY + levels * HOP_KEY + COMPUTE_KEY, piece, -1, None))
    for _, piece, distance, act in sorted(events, key=lambda event: event[:3]):
        if act is None:
            compute(piece)
        else:
            each(distance, piece, act)

    for piece in range(PIECES):
        crossing = piece >= PIECES - CROSS
        copy(0, piece, near_sem, core_sem.at[piece], core_peer, 2 * levels + (1 if crossing else levels)).wait_send()
        each_way = 2 if crossing else 1

        @pl.when(has_up & has_down)
        def _():
            copy(0, piece, far_sem, core_sem.at[piece], core_peer, each_way * (levels + 1)).wait_send()

        @pl.when(has_up != has_down)
        def _():
            copy(0, piece, far_sem, core_sem.at[piece], core_peer, each_way).wait_send()

    for batch in range(GROUPS // BATCH):
        store(batch).wait()


def main(count, raw, bandpass, whiten_taps, segment_mask, channel_block, source_block):
    segs, rows, samples = raw.shape
    channels = count * rows
    hbm = pl.BlockSpec(memory_space=pltpu.HBM)
    return pl.pallas_call(
        functools.partial(main_kernel, count),
        out_shape=jax.ShapeDtypeStruct((GROUPS // BATCH, BLOCK * rows, 128), jnp.bfloat16),
        in_specs=[hbm, hbm, hbm, hbm, hbm, pl.BlockSpec(memory_space=pltpu.SMEM), hbm],
        out_specs=hbm,
        scratch_shapes=[
            pltpu.VMEM((1, bandpass.shape[0]), bandpass.dtype),
            pltpu.VMEM(whiten_taps.shape, whiten_taps.dtype),
            pltpu.VMEM(segment_mask.shape, segment_mask.dtype),
            pltpu.VMEM((1, channels), channel_block.dtype),
            pltpu.VMEM((segs, rows, samples), jnp.bfloat16),
            pltpu.VMEM((4, samples // 2, 256), jnp.bfloat16),
            pltpu.VMEM((segs, rows, samples), jnp.float32),
            pltpu.VMEM((segs, rows, 128), jnp.float32),
            pltpu.VMEM((rows * segs, samples), jnp.float32),
            pltpu.VMEM((4, 2, rows * segs, 128), jnp.float32),
            pltpu.VMEM((PIECES, channels, GROUPS // PIECES * 256), jnp.bfloat16),
            pltpu.VMEM((GROUPS, 2, segs, 2 * rows * GROUP), jnp.float32),
            pltpu.VMEM((GROUPS, 256, 2 * rows * GROUP), jnp.bfloat16),
            pltpu.VMEM((BLOCK, channels), jnp.bfloat16),
            pltpu.VMEM((BLOCK, 2 * rows * GROUP), jnp.float32),
            pltpu.VMEM((GROUPS // BATCH, BLOCK * rows, 128), jnp.bfloat16),
            pltpu.SemaphoreType.DMA((9,)),
            pltpu.SemaphoreType.DMA((GROUPS // BATCH,)),
            pltpu.SemaphoreType.DMA((PIECES,)),
            pltpu.SemaphoreType.DMA((PIECES,)),
            pltpu.SemaphoreType.DMA((count // 2, PIECES)),
            pltpu.SemaphoreType.DMA((PIECES,)),
        ],
        compiler_params=pltpu.CompilerParams(
            collective_id=0, has_side_effects=True, vmem_limit_bytes=56 * 2**20
        ),
    )(raw, bandpass[None], whiten_taps, segment_mask, channel_block[None], source_block, jnp.asarray(dft_table()))


STEPS = 2


def lag_kernel(stacked_ref, cos_ref, sin_ref, out_ref):
    sources, rows, lags = out_ref.shape
    height, half = sources * rows, lags // 2
    re, im = (
        jnp.concatenate([stacked_ref[k] for k in range(part, stacked_ref.shape[0], 2)], axis=1) for part in range(2)
    )
    even, odd = dot(re, cos_ref[...]), dot(im, sin_ref[...])
    out_ref[:, :, half:] = (even + odd).astype(jnp.bfloat16).reshape(sources, rows, half)
    turned = 127 - iota((height, 128), 1)
    negative = even - odd
    for first in range(0, half, 128):
        part = jnp.take_along_axis(negative[:, first : first + 128], turned, axis=1)
        out_ref[:, :, half - first - 128 : half - first] = part.astype(jnp.bfloat16).reshape(sources, rows, 128)


def lag(stacked, rows):
    vmem = pl.BlockSpec(memory_space=pltpu.VMEM)
    return pl.pallas_call(
        lag_kernel,
        out_shape=jax.ShapeDtypeStruct((BLOCK, rows, LAGS), jnp.bfloat16),
        grid=(STEPS,),
        in_specs=[
            pl.BlockSpec((stacked.shape[0], BLOCK // STEPS * rows, 128), lambda i: (0, i, 0)),
            vmem,
            vmem,
        ],
        out_specs=pl.BlockSpec((BLOCK // STEPS, rows, LAGS), lambda i: (i, 0, 0)),
        compiler_params=pltpu.CompilerParams(vmem_limit_bytes=50 * 2**20),
        cost_estimate=pl.CostEstimate(flops=2 * 10**9, bytes_accessed=10**7, transcendentals=0),
    )(stacked, *(jnp.asarray(part) for part in lag_tables()))


def body(count, raw_strain, bandpass, whiten_taps, segment_mask, channel_block, source_block):
    stacked = main(count, raw_strain, bandpass, whiten_taps, segment_mask, channel_block, source_block)
    return lag(stacked, raw_strain.shape[1])


def solution(mesh):
    in_specs = (
        P(None, ("groups", "chan"), None),
        P(),
        P(("groups", "chan"), None),
        P(None, "groups"),
        P("groups"),
        P("groups"),
    )
    out_specs = P(None, ("groups", "chan"), None)
    return jax.shard_map(functools.partial(body, mesh.shape["chan"]), mesh=mesh, in_specs=in_specs, out_specs=out_specs, check_vma=False)
```
